256 devices in a mesh: layer: 4 (over y), row: 8 (over z), col: 8 (over x, core).
Axes of the slice: x: 4, y: 4, z: 8, core: 2. Of those that a mesh axis runs over, the one named last changes fastest.
Arguments:
- lower: bfloat16 [4, 4096, 12288], P('layer', 'row', 'col'), may hold values from -6 to 6
- upper: bfloat16 [4, 12288, 4096], P('layer', 'col'), may hold values from -0.02734375 to 0.02734375
- pattern: int32 [4, 32, 6], P('layer'), may hold values 0 or 1
- ancestor: float32 [4096, 4096], P('row', ('layer', 'col')), may hold values from -6 to 6
- lower_inverse: float32 [512, 512], replicated, may hold values from -2 to 2, as said below
- upper_inverse: float32 [512, 512], replicated, may hold values from -2 to 2, as said below
Outputs:
- factored: float32 [4096, 4096], P('row', ('layer', 'col'))
The draws below stay inside these ranges and needn't reach their ends.
Inputs may be any that keep to these rules, and one draw needn't show every extreme that they name: `lower_inverse`: lower triangular: zero above the diagonal, positive on it. `upper_inverse`: upper triangular: zero below the diagonal, positive on it.
All inputs are finite; a program needn't handle non-finite values. No bound on the sum of `pattern` on one device may be relied on, other than what follows from the above.
Results may differ from the reference program's by a relative error of at most 0.0003.
Values may be sent and summed in bfloat16 or wider, within the bound.
A program may use at most 128 MiB of HBM per device.

```python
import jax
import jax.numpy as jnp
from jax import lax

NA = 4096
SNW = 2048
SN = 6
NB = 512
BLK = 128
N_LAYER = 4


def draw_lower_inverse(key, part):
    key = jax.random.fold_in(key, 7)
    key_entries, key_diagonal = jax.random.split(key)
    entries = jax.random.normal(key_entries, (NB, NB), jnp.float32)
    level = NB ** (-0.25)
    diagonal = level * (1.0 + jax.random.uniform(key_diagonal, (NB,), jnp.float32))
    return jnp.tril(entries, -1) * (0.8 * level * NB ** (-0.5)) + jnp.diag(diagonal)


def draw_upper_inverse(key, part):
    key = jax.random.fold_in(key, 13)
    key_entries, key_diagonal = jax.random.split(key)
    entries = jax.random.normal(key_entries, (NB, NB), jnp.float32)
    level = NB ** (-0.25)
    diagonal = level * (1.0 + jax.random.uniform(key_diagonal, (NB,), jnp.float32))
    return jnp.triu(entries, 1) * (0.8 * level * NB ** (-0.5)) + jnp.diag(diagonal)


def with_ends(values, own_key, low, largest):
    place = [jax.random.randint(jax.random.fold_in(own_key, axis), (), 0, length) for axis, length in enumerate(values.shape)]
    longest = values.shape.index(max(values.shape))
    neighbour = place[:longest] + [(place[longest] + 1) % values.shape[longest]] + place[longest + 1:]
    return values.at[tuple(place)].set(low).at[tuple(neighbour)].set(largest)


def steps_of(own_key, extent, cuts, low, high):
    level, own = 1.0, jax.random.fold_in(own_key, 6)
    for axis_at, blocks in cuts:
        steps = jnp.exp(jax.random.uniform(jax.random.fold_in(own, axis_at), (blocks,), jnp.float32, low / len(cuts), high / len(cuts)))
        level = level * jnp.repeat(steps, extent[axis_at] // blocks).reshape([-1 if axis == axis_at else 1 for axis in range(len(extent))])
    return level


def gaussian(own_key, dims, spread, most, cuts=(), kind=jnp.bfloat16):
    loudness = steps_of(own_key, dims, cuts, -0.22, 0.18) if cuts else 1.0
    values = jax.random.normal(own_key, dims, jnp.float32) * spread * loudness
    return jnp.minimum(jnp.maximum(values, -most), most).astype(kind)


def setup_inputs(seed: int = 0) -> dict:
    arg_keys = jax.random.split(jax.random.key(seed), 7)
    lower = gaussian(arg_keys[0], (N_LAYER, NA, SN * SNW), 1.0, 6.0, ((0, 4), (1, 8), (2, 8)))
    upper = gaussian(arg_keys[1], (N_LAYER, SN * SNW, NA), (SN * SNW * N_LAYER) ** -0.5, 0.02734375, ((0, 4), (1, 8)))
    pattern = with_ends((jax.random.randint(arg_keys[2], (N_LAYER, NA // BLK, SN), 0, 4) < 3).astype(jnp.int32), jax.random.fold_in(arg_keys[2], 1), 0, 1)
    ancestor = gaussian(arg_keys[3], (NA, NA), 1.0, 6.0, ((0, 8), (1, 32)), jnp.float32)
    lower_inverse = draw_lower_inverse(jax.random.fold_in(arg_keys[6], 71), 0)
    upper_inverse = draw_upper_inverse(jax.random.fold_in(arg_keys[6], 71), 0)
    return {"lower": lower, "upper": upper, "pattern": pattern, "ancestor": ancestor, "lower_inverse": lower_inverse, "upper_inverse": upper_inverse}


def reference(lower, upper, pattern, ancestor, lower_inverse, upper_inverse):
    schur_total = jnp.zeros((NA, NA), jnp.float32)
    for layer_num in range(N_LAYER):
        keep_mask = jnp.repeat(jnp.repeat(pattern[layer_num], BLK, axis=0), SNW, axis=1).astype(jnp.bfloat16)
        kept = lower[layer_num] * keep_mask
        schur_total = schur_total + jnp.dot(kept, upper[layer_num], preferred_element_type=jnp.float32)
    frontal = ancestor - schur_total
    highest = lax.Precision.HIGHEST
    lower_panel = jnp.dot(frontal[:, :NB], upper_inverse, precision=highest)
    upper_panel = jnp.dot(lower_inverse, frontal[:NB, :], precision=highest)
    trailing = frontal - jnp.dot(lower_panel, upper_panel, precision=highest)
    row_ids = jnp.arange(NA, dtype=jnp.int32)[:, None]
    col_ids = jnp.arange(NA, dtype=jnp.int32)[None, :]
    lower_wide = jnp.pad(lower_panel, ((0, 0), (0, NA - NB)))
    upper_tall = jnp.pad(upper_panel, ((0, NA - NB), (0, 0)))
    return jnp.where(row_ids < NB, jnp.where(col_ids < NB, frontal, upper_tall), jnp.where(col_ids < NB, lower_wide, trailing))
```

```python
import math

import jax
import jax.numpy as jnp
from jax import lax
from jax.experimental import pallas as pl
from jax.experimental.pallas import tpu as pltpu
from jax.sharding import PartitionSpec as P

MESH = pl.DeviceIdType.MESH
SNW = 2048
BLK = 128
NX, NY, NZ = 4, 4, 8
ROWS = 512
HALF = 256
KS = 1536
NB = 512
ORDER = (
    (2, 2),
    (2, 1), (1, 2),
    (2, 3), (3, 2),
    (2, 0), (0, 2),
    (1, 1),
    (1, 3), (3, 1),
    (3, 3),
    (1, 0), (0, 1),
    (3, 0), (0, 3),
    (0, 0),
)
STEP = 16.0 / math.log(2.0)
TOP = 32700.0


def scale_code(x):
    top = jnp.max(jnp.abs(x), axis=0, keepdims=True)
    return jnp.ceil(jnp.log(jnp.maximum(top, 1e-30)) * STEP)


def encode(x, code):
    return jnp.round(x * (jnp.exp(code * (-1.0 / STEP)) * TOP)).astype(jnp.int32).astype(jnp.int16)


def scale_of(code):
    return jnp.exp(code * (1.0 / STEP)) * (1.0 / TOP)


def widen(q):
    return q.astype(jnp.int32).astype(jnp.float32)


def put(ref, at, x):
    n = x.shape[0]
    code = scale_code(x)
    ref[at, :n, :] = encode(x, code)
    ref[at, n:, :] = jnp.broadcast_to(code, (16, x.shape[1])).astype(jnp.int32).astype(jnp.int16)


def get(ref, at):
    n = ref.shape[1] - 16
    code = widen(ref[at, n:, :])[:1]
    return widen(ref[at, :n, :]) * scale_of(code)


def put_wide(ref, at, x):
    row = lax.broadcasted_iota(jnp.int32, (16, 128), 0) % 4
    codes = jnp.zeros((16, 128), jnp.float32)
    for g in range(4):
        part = x[:, g * 128 : (g + 1) * 128]
        code = scale_code(part)
        ref[at, g * 16 : (g + 1) * 16, :] = encode(part, code)
        codes = jnp.where(row == g, jnp.broadcast_to(code, (16, 128)), codes)
    ref[at, 64:, :] = codes.astype(jnp.int32).astype(jnp.int16)


def get_wide(ref, at):
    scales = scale_of(widen(ref[at, 64:, :]))
    return [widen(ref[at, g * 16 : (g + 1) * 16, :]) * scales[g : g + 1] for g in range(4)]


def split(x):
    hi = x.astype(jnp.bfloat16)
    return hi, (x - hi.astype(jnp.float32)).astype(jnp.bfloat16)


def dot3(a, b):
    (ah, al), (bh, bl) = a, b
    dot = lambda u, v: jnp.dot(u, v, preferred_element_type=jnp.float32)
    return dot(ah, bh) + (dot(ah, bl) + dot(al, bh))


def kernel(
    pattern, lower, upper, ancestor, linv, uinv, out,
    a_ref, b_ref, bp_ref, anc, lin, uin, parts, peer,
    ms, mr, ns, nr, zs, zr,
    pp, px, ps, pr, ags, agr, agp, fp, wh, wl,
    in_sem, b_sem, d_ss, d_rs, m_ss, m_rs, n_ss, n_rs, z_ss, z_rs,
    px_sem, p_ss, p_rs, ag_ss, ag_rs, agp_sem,
):
    y, z, col = (lax.axis_index(k) for k in ("layer", "row", "col"))
    x, c = col // 2, col % 2
    other = 1 - c
    inner = z > 0

    def dev(dy, dx):
        return (lax.rem(y + dy + 4, 4), z, lax.rem(x + dx + 4, 4) * 2 + c)

    def dev_a(d):
        return dev(c * d, other * d)

    def dev_b(d):
        return dev(other * d, c * d)

    twin = (y, z, x * 2 + other)

    loads = [
        pltpu.make_async_copy(lower.at[0], a_ref, in_sem.at[0]),
        pltpu.make_async_copy(ancestor, anc, in_sem.at[1]),
        pltpu.make_async_copy(uinv, uin, in_sem.at[2]),
        pltpu.make_async_copy(linv, lin, in_sem.at[3]),
    ]
    b_loads = []
    for k, (dy, dx) in enumerate(ORDER):
        first = lax.rem(y + dy, 4) * 1024 + lax.rem(x + dx, 4) * 256
        b_loads.append(
            pltpu.make_async_copy(
                upper.at[0, :, pl.ds(pl.multiple_of(first, 256), 256)], b_ref.at[k], b_sem.at[k]
            )
        )
    bp_loads = [
        pltpu.make_async_copy(upper.at[0, :, q * 256 : (q + 1) * 256], bp_ref.at[q], b_sem.at[16 + q])
        for q in range(2)
    ]
    loads[0].start()

    @pl.when(inner)
    def _():
        for cp in bp_loads:
            cp.start()

    loads[1].start()
    for cp in b_loads:
        cp.start()
    loads[2].start()
    loads[3].start()

    barrier = pltpu.get_barrier_semaphore()
    pl.semaphore_signal(barrier, inc=1, device_id=twin, device_id_type=MESH)
    for i in range(1, 16):
        pl.semaphore_signal(barrier, inc=1, device_id=dev(i // 4, i % 4), device_id_type=MESH)
    for i in range(1, NZ):
        pl.semaphore_signal(
            barrier, inc=1, device_id=(y, lax.rem(z + i, NZ), col), device_id_type=MESH
        )

    loads[0].wait()
    for rb in range(ROWS // BLK):
        for kb in range(KS // 512):
            node = (col * KS + kb * 512) // SNW
            keep = pattern[0, z * (ROWS // BLK) + rb, node].astype(jnp.float32)
            at = (slice(rb * BLK, (rb + 1) * BLK), slice(kb * 512, (kb + 1) * 512))
            a_ref[at] = (a_ref[at].astype(jnp.float32) * keep).astype(jnp.bfloat16)

    loads[1].wait()

    @pl.when(inner)
    def _():
        for q in range(2):
            bp_loads[q].wait()
            pp[:, q * 256 : (q + 1) * 256] = jnp.dot(
                a_ref[...], bp_ref[q], preferred_element_type=jnp.float32
            )

        @pl.when((y == 0) & (col < 4))
        def _():
            here = pl.ds(pl.multiple_of(col * 128, 128), 128)
            pp[:, here] -= anc[...]

    pl.semaphore_wait(barrier, 23)

    px_copy = pltpu.make_async_remote_copy(
        src_ref=pp.at[pl.ds(pl.multiple_of(other * HALF, HALF), HALF)],
        dst_ref=px,
        send_sem=px_sem.at[0],
        recv_sem=px_sem.at[1],
        device_id=twin,
        device_id_type=MESH,
    )

    @pl.when(inner)
    def _():
        px_copy.start()

    def p_copy(i):
        return pltpu.make_async_remote_copy(
            src_ref=ps.at[i],
            dst_ref=pr.at[i],
            send_sem=p_ss.at[i],
            recv_sem=p_rs.at[i],
            device_id=dev(i // 4, i % 4),
            device_id_type=MESH,
        )

    def ag_copy(i):
        return pltpu.make_async_remote_copy(
            src_ref=ags.at[0],
            dst_ref=agr.at[i],
            send_sem=ag_ss.at[i],
            recv_sem=ag_rs.at[i],
            device_id=dev(i // 4, i % 4),
            device_id_type=MESH,
        )

    agp_copy = pltpu.make_async_remote_copy(
        src_ref=agr,
        dst_ref=agp,
        send_sem=agp_sem.at[0],
        recv_sem=agp_sem.at[1],
        device_id=twin,
        device_id_type=MESH,
    )

    def chip_at(i):
        return lax.rem(y + i // 4, 4) * 4 + lax.rem(x + i % 4, 4)

    def chip_from(i):
        return lax.rem(y + 4 - i // 4, 4) * 4 + lax.rem(x + 4 - i % 4, 4)

    def panel_slice(i):
        j = chip_at(i)
        mine = pp[pl.ds(pl.multiple_of(c * HALF + j * 16, 16), 16), :]
        return mine + px[pl.ds(pl.multiple_of(j * 16, 16), 16), :]

    def panel_send():
        @pl.when(inner)
        def _():
            px_copy.wait_recv()

            def body(i, carry):
                put_wide(ps, i, panel_slice(i))
                p_copy(i).start()
                return carry

            lax.fori_loop(1, 16, body, 0)

    def panel_sum():
        @pl.when(inner)
        def _():
            mine = panel_slice(0)

            def body(i, total):
                p_copy(i).wait_recv()
                return total + jnp.concatenate(get_wide(pr, i), axis=1)

            total = lax.fori_loop(1, 16, body, mine)
            put_wide(ags, 0, -total)
            agr[0] = ags[0]

            def send(i, carry):
                ag_copy(i).start()
                return carry

            lax.fori_loop(1, 16, send, 0)

    def panel_gather():
        @pl.when(inner)
        def _():
            def body(i, carry):
                ag_copy(i).wait_recv()
                return carry

            lax.fori_loop(1, 16, body, 0)
            agp_copy.start()

    def panel_use():
        @pl.when(inner)
        def _():
            def unpack(ref, half):
                def body(i, carry):
                    at = pl.multiple_of(half * HALF + chip_from(i) * 16, 16)
                    for g, part in enumerate(get_wide(ref, i)):
                        fp[pl.ds(at, 16), g * 128 : (g + 1) * 128] = part
                    return carry

                lax.fori_loop(0, 16, body, 0)

            unpack(agr, c)
            agp_copy.wait_recv()
            unpack(agp, other)
            loads[2].wait()
            loads[3].wait()
            panel = dot3(split(fp[...]), split(uin[...]))
            fp[...] = panel
            w = dot3(split(panel), split(lin[...]))
            wh[...], wl[...] = split(w)

    def slots(k):
        dy, dx = ORDER[k]
        return dx * 4 + dy, dy * 4 + dx

    def d_copy(k):
        s0, s1 = slots(k)
        s = jnp.where(c == 0, s1, s0)
        return pltpu.make_async_remote_copy(
            src_ref=parts.at[other, s],
            dst_ref=peer.at[s],
            send_sem=d_ss.at[s],
            recv_sem=d_rs.at[s],
            device_id=twin,
            device_id_type=MESH,
        )

    def compute(k):
        s0, s1 = slots(k)
        b_loads[k].wait()
        both = jnp.dot(a_ref[...], b_ref[k], preferred_element_type=jnp.float32)
        parts[0, s0] = both[:, :128]
        parts[1, s1] = both[:, 128:]
        d_copy(k).start()

    def arrived(da, db):
        s = da * 4 + db
        pltpu.make_async_copy(peer.at[s], peer.at[s], d_rs.at[s]).wait()
        parts[c, s] += peer[s]

    def rows(h):
        return slice(h * HALF, (h + 1) * HALF)

    def m_copy(kind, way, db):
        at = kind * 8 + way * 4 + db
        return pltpu.make_async_remote_copy(
            src_ref=ms.at[at],
            dst_ref=mr.at[at],
            send_sem=m_ss.at[at],
            recv_sem=m_rs.at[at],
            device_id=dev_a(1 if way == 0 else -1),
            device_id_type=MESH,
        )

    def m_send(kind, way, da, db, h, add=None):
        value = parts[c, da * 4 + db, rows(h), :]
        if add is not None:
            m_copy(*add).wait_recv()
            value = value + get(mr, add[0] * 8 + add[1] * 4 + add[2])
        put(ms, kind * 8 + way * 4 + db, value)
        m_copy(kind, way, db).start()

    def m1(db):
        arrived(2, db)
        m_send(0, 0, 2, db, 0)
        m_send(0, 1, 2, db, 1)

    def m2p(db):
        arrived(1, db)
        m_send(1, 0, 1, db, 1)

    def m2m(db):
        arrived(3, db)
        m_send(1, 1, 3, db, 0)

    def m3(db):
        m_send(2, 0, 1, db, 0, add=(0, 0, db))
        m_send(2, 1, 3, db, 1, add=(0, 1, db))

    def n_copy(d, h):
        at = (d - 1) * 2 + h
        return pltpu.make_async_remote_copy(
            src_ref=ns.at[at],
            dst_ref=nr.at[at],
            send_sem=n_ss.at[at],
            recv_sem=n_rs.at[at],
            device_id=dev_b(d),
            device_id_type=MESH,
        )

    def first_sum(db, h):
        total = parts[c, db, rows(h), :]
        for kind, way in ((2, 0), (1, 1)) if h == 0 else ((1, 0), (2, 1)):
            m_copy(kind, way, db).wait_recv()
            total = total + get(mr, kind * 8 + way * 4 + db)
        return total

    def n_send(db):
        arrived(0, db)
        for h in range(2):
            put(ns, (db - 1) * 2 + h, first_sum(db, h))
            n_copy(db, h).start()

    compute(0)
    compute(1)
    compute(2)
    m1(2)
    panel_send()
    compute(3)
    compute(4)
    m1(1)
    m2p(2)
    compute(5)
    compute(6)
    m1(3)
    m2m(2)
    compute(7)
    m1(0)
    compute(8)
    compute(9)
    m2p(1)
    m3(2)
    compute(10)
    m2p(3)
    m2m(1)
    m3(1)
    compute(11)
    compute(12)
    m2m(3)
    m3(3)
    compute(13)
    compute(14)
    m2p(0)
    panel_sum()
    compute(15)
    m2m(0)
    m3(0)
    n_send(2)
    n_send(1)
    n_send(3)
    arrived(0, 0)

    def z_copy(d, h):
        at = d * 2 + h
        return pltpu.make_async_remote_copy(
            src_ref=zs.at[h],
            dst_ref=zr.at[h],
            send_sem=z_ss.at[at],
            recv_sem=z_rs.at[h],
            device_id=(y, d, col),
            device_id_type=MESH,
        )

    def final_sum(h):
        total = first_sum(0, h)
        for d in (1, 3, 2):
            n_copy(d, h).wait_recv()
            total = total + get(nr, (d - 1) * 2 + h)
        return anc[rows(h), :] - total

    panel_gather()
    panel_use()
    for h in range(2):
        out[rows(h), :] = final_sum(h)

        @pl.when(z == 0)
        def _():
            put(zs, h, out[rows(h), :])
            for d in (4, 3, 5, 2, 6, 1, 7):
                z_copy(d, h).start()

    in_panel = (y == 0) & (col < 4)

    @pl.when(z == 0)
    def _():
        loads[2].wait()
        loads[3].wait()

        @pl.when(jnp.logical_not(in_panel))
        def _():
            out[...] = dot3(split(lin[...]), split(out[...]))

        for h in range(2):
            for d in range(1, NZ):
                z_copy(d, h).wait_send()

    @pl.when(inner)
    def _():
        z_copy(0, 0).wait_recv()
        z_copy(0, 1).wait_recv()

        @pl.when(in_panel)
        def _():
            out[...] = fp[:, pl.ds(pl.multiple_of(col * 128, 128), 128)]

        @pl.when(jnp.logical_not(in_panel))
        def _():
            for h in range(2):
                w = (wh[:, rows(h)], wl[:, rows(h)])
                out[...] -= dot3(w, split(get(zr, h)))

        px_copy.wait_send()
        agp_copy.wait_send()

        def sent(i, carry):
            p_copy(i).wait_send()
            ag_copy(i).wait_send()
            return carry

        lax.fori_loop(1, 16, sent, 0)

    for k in range(16):
        d_copy(k).wait_send()
    for at in range(24):
        m_copy(at // 8, at // 4 % 2, at % 4).wait_send()
    for d in range(1, 4):
        for h in range(2):
            n_copy(d, h).wait_send()


def shards(lower, upper, pattern, ancestor, lower_inverse, upper_inverse):
    f32, bf16, i16 = jnp.float32, jnp.bfloat16, jnp.int16
    vmem, dma = pltpu.VMEM, pltpu.SemaphoreType.DMA
    hbm = pl.BlockSpec(memory_space=pl.ANY)
    msg = HALF + 16
    return pl.pallas_call(
        kernel,
        out_shape=jax.ShapeDtypeStruct((ROWS, 128), f32),
        in_specs=[pl.BlockSpec(memory_space=pltpu.SMEM)] + [hbm] * 5,
        out_specs=pl.BlockSpec(memory_space=pltpu.VMEM),
        scratch_shapes=[
            vmem((ROWS, KS), bf16),
            vmem((16, KS, 256), bf16),
            vmem((2, KS, 256), bf16),
            vmem((ROWS, 128), f32),
            vmem((NB, NB), f32),
            vmem((NB, NB), f32),
            vmem((2, 16, ROWS, 128), f32),
            vmem((16, ROWS, 128), f32),
            vmem((24, msg, 128), i16),
            vmem((24, msg, 128), i16),
            vmem((6, msg, 128), i16),
            vmem((6, msg, 128), i16),
            vmem((2, msg, 128), i16),
            vmem((2, msg, 128), i16),
            vmem((ROWS, NB), f32),
            vmem((HALF, NB), f32),
            vmem((16, 80, 128), i16),
            vmem((16, 80, 128), i16),
            vmem((1, 80, 128), i16),
            vmem((16, 80, 128), i16),
            vmem((16, 80, 128), i16),
            vmem((ROWS, NB), f32),
            vmem((ROWS, NB), bf16),
            vmem((ROWS, NB), bf16),
            dma((4,)),
            dma((18,)),
            dma((16,)),
            dma((16,)),
            dma((24,)),
            dma((24,)),
            dma((6,)),
            dma((6,)),
            dma((16,)),
            dma((2,)),
            dma((2,)),
            dma((16,)),
            dma((16,)),
            dma((16,)),
            dma((16,)),
            dma((2,)),
        ],
        compiler_params=pltpu.CompilerParams(
            collective_id=0, has_side_effects=True, vmem_limit_bytes=56 * 2**20
        ),
    )(pattern, lower, upper, ancestor, lower_inverse, upper_inverse)


def solution(mesh):
    in_specs = (
        P("layer", "row", "col"),
        P("layer", "col", None),
        P("layer", None, None),
        P("row", ("layer", "col")),
        P(),
        P(),
    )
    out_specs = P("row", ("layer", "col"))
    return jax.shard_map(shards, mesh=mesh, in_specs=in_specs, out_specs=out_specs, check_vma=False)
```

```python
import math

import jax
import jax.numpy as jnp
from jax import lax
from jax.experimental import pallas as pl
from jax.experimental.pallas import tpu as pltpu
from jax.sharding import PartitionSpec as P

MESH = pl.DeviceIdType.MESH
SNW = 2048
BLK = 128
NX, NY, NZ = 4, 4, 8
ROWS = 512
HALF = 256
QUARTER = 128
KS = 1536
NB = 512
ORDER = (
    (2, 2),
    (2, 1), (1, 2),
    (2, 3), (3, 2),
    (2, 0), (0, 2),
    (1, 1), (3, 3),
    (1, 3), (3, 1),
    (1, 0), (0, 1),
    (3, 0), (0, 3),
    (0, 0),
)
STEP = 16.0 / math.log(2.0)
TOP = 32700.0


def scale_code(x):
    top = jnp.max(jnp.abs(x), axis=0, keepdims=True)
    return jnp.ceil(jnp.log(jnp.maximum(top, 1e-30)) * STEP)


def encode(x, code):
    return jnp.round(x * (jnp.exp(code * (-1.0 / STEP)) * TOP)).astype(jnp.int32).astype(jnp.int16)


def scale_of(code):
    return jnp.exp(code * (1.0 / STEP)) * (1.0 / TOP)


def widen(q):
    return q.astype(jnp.int32).astype(jnp.float32)


def put(ref, at, x):
    n = x.shape[0]
    code = scale_code(x)
    ref[at, :n, :] = encode(x, code)
    ref[at, n:, :] = jnp.broadcast_to(code, (16, x.shape[1])).astype(jnp.int32).astype(jnp.int16)


def get(ref, at):
    n = ref.shape[1] - 16
    code = widen(ref[at, n:, :])[:1]
    return widen(ref[at, :n, :]) * scale_of(code)


def put_wide(ref, at, x):
    row = lax.broadcasted_iota(jnp.int32, (16, 128), 0) % 4
    codes = jnp.zeros((16, 128), jnp.float32)
    for g in range(4):
        part = x[:, g * 128 : (g + 1) * 128]
        code = scale_code(part)
        ref[at, g * 16 : (g + 1) * 16, :] = encode(part, code)
        codes = jnp.where(row == g, jnp.broadcast_to(code, (16, 128)), codes)
    ref[at, 64:, :] = codes.astype(jnp.int32).astype(jnp.int16)


def get_wide(ref, at):
    scales = scale_of(widen(ref[at, 64:, :]))
    return [widen(ref[at, g * 16 : (g + 1) * 16, :]) * scales[g : g + 1] for g in range(4)]


def split(x):
    hi = x.astype(jnp.bfloat16)
    return hi, (x - hi.astype(jnp.float32)).astype(jnp.bfloat16)


def dot3(a, b):
    (ah, al), (bh, bl) = a, b
    dot = lambda u, v: jnp.dot(u, v, preferred_element_type=jnp.float32)
    return dot(ah, bh) + (dot(ah, bl) + dot(al, bh))


def kernel(
    pattern, lower, upper, ancestor, linv, uinv, out,
    a_ref, b_ref, bp_ref, anc, lin, uin, parts, peer,
    ms, mr, ns, nr, zs, zr,
    pp, px, ps, pr, ags, agr, agp, fp, wh, wl,
    in_sem, b_sem, d_ss, d_rs, m_ss, m_rs, n_ss, n_rs, z_ss, z_rs,
    px_sem, p_ss, p_rs, ag_ss, ag_rs, agp_sem, corner, token,
):
    y, z, col = (lax.axis_index(k) for k in ("layer", "row", "col"))
    x, c = col >> 1, col & 1
    other = 1 - c
    inner = z > 0

    def dev(dy, dx):
        return ((y + dy) & 3, z, ((x + dx) & 3) * 2 + c)

    near_a = {d: dev(c * d, other * d) for d in (1, -1)}
    near_b = {d: dev(other * d, c * d) for d in (1, 2, 3)}

    twin = (y, z, x * 2 + other)

    up, down = (y, (z + 1) & (NZ - 1), col), (y, (z - 1) & (NZ - 1), col)

    loads = [
        pltpu.make_async_copy(lower.at[0], a_ref, in_sem.at[0]),
        pltpu.make_async_copy(ancestor, anc, in_sem.at[1]),
        pltpu.make_async_copy(uinv, uin, in_sem.at[2]),
        pltpu.make_async_copy(linv, lin, in_sem.at[3]),
    ]
    b_loads = []
    for k, (dy, dx) in enumerate(ORDER):
        first = ((y + dy) & 3) * 1024 + ((x + dx) & 3) * 256
        b_loads.append(
            pltpu.make_async_copy(
                upper.at[0, :, pl.ds(pl.multiple_of(first, 256), 256)], b_ref.at[k], b_sem.at[k]
            )
        )
    bp_loads = [
        pltpu.make_async_copy(upper.at[0, :, q * 256 : (q + 1) * 256], bp_ref.at[q], b_sem.at[16 + q])
        for q in range(2)
    ]
    loads[0].start()

    @pl.when(inner)
    def _():
        for cp in bp_loads:
            cp.start()

    loads[1].start()
    for cp in b_loads:
        cp.start()
    loads[2].start()
    loads[3].start()

    barrier = pltpu.get_barrier_semaphore()
    partners = [twin] + [dev(0, d) for d in (1, 2, 3)] + [dev(d, 0) for d in (1, 2, 3)]
    partners += [up, down]
    for partner in partners:
        pl.semaphore_signal(barrier, inc=1, device_id=partner, device_id_type=MESH)

    loads[0].wait()
    for rb in range(ROWS // BLK):
        for kb in range(KS // 512):
            node = (col * KS + kb * 512) // SNW
            keep = pattern[node, 0, z * (ROWS // BLK) + rb].astype(jnp.float32)
            at = (slice(rb * BLK, (rb + 1) * BLK), slice(kb * 512, (kb + 1) * 512))
            a_ref[at] = (a_ref[at].astype(jnp.float32) * keep).astype(jnp.bfloat16)

    loads[1].wait()

    @pl.when(inner)
    def _():
        for q in range(2):
            bp_loads[q].wait()
        for q in range(2):
            pp[:, q * 256 : (q + 1) * 256] = jnp.dot(
                a_ref[...], bp_ref[q], preferred_element_type=jnp.float32
            )

        @pl.when((y == 0) & (col < 4))
        def _():
            here = pl.ds(pl.multiple_of(col * 128, 128), 128)
            pp[:, here] -= anc[...]


    px_copy = pltpu.make_async_remote_copy(
        src_ref=pp.at[pl.ds(pl.multiple_of(other * HALF, HALF), HALF)],
        dst_ref=px,
        send_sem=px_sem.at[0],
        recv_sem=px_sem.at[1],
        device_id=twin,
        device_id_type=MESH,
    )

    def enter():
        pl.semaphore_wait(barrier, len(partners))

        @pl.when(inner)
        def _():
            px_copy.start()
            for d in (1, 2, 3):
                pl.semaphore_signal(corner, inc=1, device_id=dev(0, d), device_id_type=MESH)

    def pass_token():
        @pl.when((z == 1) | (z == 2) | (z == 3) | (z == 6) | (z == 7))
        def _():
            pl.semaphore_wait(token, 1)

        @pl.when((z >= 1) & (z <= 4))
        def _():
            pl.semaphore_signal(token, inc=1, device_id=down, device_id_type=MESH)

        @pl.when(z >= 5)
        def _():
            pl.semaphore_signal(token, inc=1, device_id=up, device_id_type=MESH)

    def p_copy(i):
        return pltpu.make_async_remote_copy(
            src_ref=ps.at[chip_at(i)],
            dst_ref=pr.at[i],
            send_sem=p_ss.at[i],
            recv_sem=p_rs.at[i],
            device_id=dev(i // 4, i % 4),
            device_id_type=MESH,
        )

    def ag_copy(i):
        return pltpu.make_async_remote_copy(
            src_ref=ags.at[0],
            dst_ref=agr.at[i],
            send_sem=ag_ss.at[i],
            recv_sem=ag_rs.at[i],
            device_id=dev(i // 4, i % 4),
            device_id_type=MESH,
        )

    agp_copy = pltpu.make_async_remote_copy(
        src_ref=agr,
        dst_ref=agp,
        send_sem=agp_sem.at[0],
        recv_sem=agp_sem.at[1],
        device_id=twin,
        device_id_type=MESH,
    )

    def chip_at(i):
        return ((y + i // 4) & 3) * 4 + ((x + i % 4) & 3)

    def chip_from(i):
        return ((y - i // 4) & 3) * 4 + ((x - i % 4) & 3)

    def panel_send():
        @pl.when(inner)
        def _():
            px_copy.wait_recv()
            pl.semaphore_wait(corner, 3)
            mine = pp[pl.ds(pl.multiple_of(c * HALF, HALF), HALF), :] + px[...]
            px[...] = mine
            for j in range(16):
                put_wide(ps, j, mine[j * 16 : (j + 1) * 16])
            for i in range(1, 16):
                p_copy(i).start()

    def panel_sum():
        @pl.when(inner)
        def _():
            for i in range(1, 16):
                p_copy(i).wait_recv()
            total = px[pl.ds(pl.multiple_of(chip_at(0) * 16, 16), 16), :]
            for i in range(1, 16):
                total = total + jnp.concatenate(get_wide(pr, i), axis=1)
            put_wide(ags, 0, -total)
            agr[0] = ags[0]
            for i in range(1, 16):
                ag_copy(i).start()

    def panel_gather():
        @pl.when(inner)
        def _():
            for i in range(1, 16):
                ag_copy(i).wait_recv()
            agp_copy.start()

    def panel_use():
        @pl.when(inner)
        def _():
            def unpack(ref, half):
                for i in range(16):
                    at = pl.multiple_of(half * HALF + chip_from(i) * 16, 16)
                    for g, part in enumerate(get_wide(ref, i)):
                        fp[pl.ds(at, 16), g * 128 : (g + 1) * 128] = part

            unpack(agr, c)
            agp_copy.wait_recv()
            unpack(agp, other)
            loads[2].wait()
            loads[3].wait()
            panel = dot3(split(fp[...]), split(uin[...]))
            fp[...] = panel
            w = dot3(split(panel), split(lin[...]))
            wh[...], wl[...] = split(w)

    def slots(k):
        dy, dx = ORDER[k]
        return dx * 4 + dy, dy * 4 + dx

    def d_copy(k):
        s0, s1 = slots(k)
        s = jnp.where(c == 0, s1, s0)
        return pltpu.make_async_remote_copy(
            src_ref=parts.at[other, s],
            dst_ref=peer.at[s],
            send_sem=d_ss.at[s],
            recv_sem=d_rs.at[s],
            device_id=twin,
            device_id_type=MESH,
        )

    def compute(*ks):
        for k in ks:
            b_loads[k].wait()
        tiles = 2 // len(ks)
        for k in ks:
            s0, s1 = slots(k)
            for t in range(tiles):
                at = slice(t * ROWS // tiles, (t + 1) * ROWS // tiles)
                both = jnp.dot(a_ref[at], b_ref[k], preferred_element_type=jnp.float32)
                parts[0, s0, at] = both[:, :128]
                parts[1, s1, at] = both[:, 128:]

    def step(*ks):
        compute(*ks)
        for k in ks:
            d_copy(k).start()

    here = set()

    def arrive(da, db):
        s = da * 4 + db
        if s not in here:
            here.add(s)
            pltpu.make_async_copy(peer.at[s], peer.at[s], d_rs.at[s]).wait()

    def chip_sum(da, db, at):
        s = da * 4 + db
        return parts[c, s, at, :] + peer[s, at, :]

    def rows(h):
        return slice(h * HALF, (h + 1) * HALF)

    def quarter(h, q):
        return slice(h * HALF + q * QUARTER, h * HALF + (q + 1) * QUARTER)

    def m_at(kind, way, h, db):
        return ((kind * 2 + way) * 2 + h) * 4 + db

    def m_copy(kind, way, h, db):
        at = m_at(kind, way, h, db)
        return pltpu.make_async_remote_copy(
            src_ref=ms.at[at],
            dst_ref=mr.at[at],
            send_sem=m_ss.at[at],
            recv_sem=m_rs.at[at],
            device_id=near_a[1 if way == 0 else -1],
            device_id_type=MESH,
        )

    def m1(h, db):
        return [(0, 0, h, 2, db, 0), (0, 1, h, 2, db, 1)]

    def m2(h, db):
        return [(1, 0, h, 1, db, 1), (1, 1, h, 3, db, 0)]

    def m3(h, db):
        return [(2, 0, h, 1, db, 0), (2, 1, h, 3, db, 1)]

    def send(*groups):
        group = [m for g in groups for m in g]
        for kind, way, h, da, db, q in group:
            arrive(da, db)
            if kind == 2:
                m_copy(0, way, h, db).wait_recv()
        for kind, way, h, da, db, q in group:
            value = chip_sum(da, db, quarter(h, q))
            if kind == 2:
                value = value + get(mr, m_at(0, way, h, db))
            put(ms, m_at(kind, way, h, db), value)
        for kind, way, h, da, db, q in group:
            m_copy(kind, way, h, db).start()

    def n_copy(d, h):
        at = (d - 1) * 2 + h
        return pltpu.make_async_remote_copy(
            src_ref=ns.at[at],
            dst_ref=nr.at[at],
            send_sem=n_ss.at[at],
            recv_sem=n_rs.at[at],
            device_id=near_b[d],
            device_id_type=MESH,
        )

    sources = (((2, 0), (1, 1)), ((1, 0), (2, 1)))

    def first_wait(db, h):
        arrive(0, db)
        for q in range(2):
            for kind, way in sources[q]:
                m_copy(kind, way, h, db).wait_recv()

    def first_sum(db, h):
        sums = []
        for q in range(2):
            total = chip_sum(0, db, quarter(h, q))
            for kind, way in sources[q]:
                total = total + get(mr, m_at(kind, way, h, db))
            sums.append(total)
        return jnp.concatenate(sums, axis=0)

    def n_send(h, *dbs):
        for db in dbs:
            first_wait(db, h)
        for db in dbs:
            put(ns, (db - 1) * 2 + h, first_sum(db, h))
        for db in dbs:
            n_copy(db, h).start()

    compute(0)
    compute(1, 2)
    compute(3, 4)
    enter()
    for k in range(5):
        d_copy(k).start()
    step(5, 6)
    panel_send()
    send(m1(0, 2), m1(1, 2))
    send(m1(0, 1), m1(0, 3))
    step(7, 8)
    send(m1(0, 0), m2(0, 2))
    step(9, 10)
    pass_token()
    send(m1(1, 1), m1(1, 3))
    send(m2(0, 1), m2(0, 3))
    step(11, 12)
    send(m3(0, 2), m1(1, 0))
    step(13, 14)
    send(m3(0, 1), m3(0, 3))
    step(15)
    send(m2(0, 0), m2(1, 2))
    send(m3(0, 0), m2(1, 1), m2(1, 3))
    panel_sum()
    send(m3(1, 2))
    n_send(0, 2)
    send(m3(1, 1), m3(1, 3))
    n_send(0, 1, 3)
    send(m2(1, 0), m3(1, 0))
    n_send(1, 2)
    n_send(1, 1, 3)

    def z_copy(d, h):
        at = d * 2 + h
        return pltpu.make_async_remote_copy(
            src_ref=zs.at[h],
            dst_ref=zr.at[h],
            send_sem=z_ss.at[at],
            recv_sem=z_rs.at[h],
            device_id=(y, d, col),
            device_id_type=MESH,
        )

    def final_sum(h):
        first_wait(0, h)
        for d in (1, 2, 3):
            n_copy(d, h).wait_recv()
        total = first_sum(0, h)
        for d in (1, 2, 3):
            total = total + get(nr, (d - 1) * 2 + h)
        return anc[rows(h), :] - total

    for h in range(2):
        out[rows(h), :] = final_sum(h)

        @pl.when(z == 0)
        def _():
            put(zs, h, out[rows(h), :])
            if h == 0:
                pl.semaphore_wait(token, 2)
            for d in (4, 3, 5, 2, 6, 1, 7):
                z_copy(d, h).start()

    panel_gather()
    panel_use()
    in_panel = (y == 0) & (col < 4)

    @pl.when(z == 0)
    def _():
        loads[2].wait()
        loads[3].wait()

        @pl.when(jnp.logical_not(in_panel))
        def _():
            out[...] = dot3(split(lin[...]), split(out[...]))

        for h in range(2):
            for d in range(1, NZ):
                z_copy(d, h).wait_send()

    @pl.when(inner)
    def _():
        @pl.when(in_panel)
        def _():
            for h in range(2):
                z_copy(0, h).wait_recv()
            out[...] = fp[:, pl.ds(pl.multiple_of(col * 128, 128), 128)]

        @pl.when(jnp.logical_not(in_panel))
        def _():
            for h in range(2):
                z_copy(0, h).wait_recv()
                w = (wh[:, rows(h)], wl[:, rows(h)])
                out[...] -= dot3(w, split(get(zr, h)))

        px_copy.wait_send()
        agp_copy.wait_send()

        for i in range(1, 16):
            p_copy(i).wait_send()
            ag_copy(i).wait_send()

    for k in range(16):
        d_copy(k).wait_send()
    for at in range(48):
        m_copy(at // 16, at // 8 % 2, at // 4 % 2, at % 4).wait_send()
    for d in range(1, 4):
        for h in range(2):
            n_copy(d, h).wait_send()


def shards(lower, upper, pattern, ancestor, lower_inverse, upper_inverse):
    f32, bf16, i16 = jnp.float32, jnp.bfloat16, jnp.int16
    vmem, dma = pltpu.VMEM, pltpu.SemaphoreType.DMA
    hbm = pl.BlockSpec(memory_space=pl.ANY)
    msg = HALF + 16
    return pl.pallas_call(
        kernel,
        out_shape=pltpu.VMEM((ROWS, 128), f32),
        in_specs=[pl.BlockSpec(memory_space=pltpu.SMEM)] + [hbm] * 5,
        out_specs=pl.BlockSpec(memory_space=pltpu.VMEM),
        scratch_shapes=[
            vmem((ROWS, KS), bf16),
            vmem((16, KS, 256), bf16),
            vmem((2, KS, 256), bf16),
            vmem((ROWS, 128), f32),
            vmem((NB, NB), f32),
            vmem((NB, NB), f32),
            vmem((2, 16, ROWS, 128), f32),
            vmem((16, ROWS, 128), f32),
            vmem((48, QUARTER + 16, 128), i16),
            vmem((48, QUARTER + 16, 128), i16),
            vmem((6, msg, 128), i16),
            vmem((6, msg, 128), i16),
            vmem((2, msg, 128), i16),
            vmem((2, msg, 128), i16),
            vmem((ROWS, NB), f32),
            vmem((HALF, NB), f32),
            vmem((16, 80, 128), i16),
            vmem((16, 80, 128), i16),
            vmem((1, 80, 128), i16),
            vmem((16, 80, 128), i16),
            vmem((16, 80, 128), i16),
            vmem((ROWS, NB), f32),
            vmem((ROWS, NB), bf16),
            vmem((ROWS, NB), bf16),
            dma((4,)),
            dma((18,)),
            dma((16,)),
            dma((16,)),
            dma((48,)),
            dma((48,)),
            dma((6,)),
            dma((6,)),
            dma((16,)),
            dma((2,)),
            dma((2,)),
            dma((16,)),
            dma((16,)),
            dma((16,)),
            dma((16,)),
            dma((2,)),
            pltpu.SemaphoreType.REGULAR,
            pltpu.SemaphoreType.REGULAR,
        ],
        compiler_params=pltpu.CompilerParams(
            collective_id=0, has_side_effects=True, vmem_limit_bytes=56 * 2**20
        ),
    )(jnp.transpose(pattern, (2, 0, 1)), lower, upper, ancestor, lower_inverse, upper_inverse)


def solution(mesh):
    in_specs = (
        P("layer", "row", "col"),
        P("layer", "col", None),
        P("layer", None, None),
        P("row", ("layer", "col")),
        P(),
        P(),
    )
    out_specs = P("row", ("layer", "col"))
    return jax.shard_map(shards, mesh=mesh, in_specs=in_specs, out_specs=out_specs, check_vma=False)
```

```python
import math

import jax
import jax.numpy as jnp
from jax import lax
from jax.experimental import pallas as pl
from jax.experimental.pallas import tpu as pltpu
from jax.sharding import PartitionSpec as P

MESH = pl.DeviceIdType.MESH
SNW = 2048
BLK = 128
NX, NY, NZ = 4, 4, 8
ROWS = 512
HALF = 256
QUARTER = 128
KS = 1536
NB = 512
ORDER = (
    (2, 2),
    (2, 1), (1, 2),
    (2, 3), (3, 2),
    (2, 0), (0, 2),
    (1, 1), (3, 3),
    (1, 3), (3, 1),
    (1, 0), (0, 1),
    (3, 0), (0, 3),
    (0, 0),
)
FIRST = (3, 5, 1, 7)
FAR = (4, 3, 5, 2, 6, 1, 7)
STEP = 16.0 / math.log(2.0)
TOP = 32700.0


def scale_code(x):
    top = jnp.max(jnp.abs(x), axis=0, keepdims=True)
    return jnp.ceil(jnp.log(jnp.maximum(top, 1e-30)) * STEP)


def encode(x, code):
    return jnp.round(x * (jnp.exp(code * (-1.0 / STEP)) * TOP)).astype(jnp.int32).astype(jnp.int16)


def scale_of(code):
    return jnp.exp(code * (1.0 / STEP)) * (1.0 / TOP)


def widen(q):
    return q.astype(jnp.int32).astype(jnp.float32)


def put(ref, at, x):
    n = x.shape[0]
    code = scale_code(x)
    ref[at, :n, :] = encode(x, code)
    ref[at, n:, :] = jnp.broadcast_to(code, (16, x.shape[1])).astype(jnp.int32).astype(jnp.int16)


def get(ref, at):
    n = ref.shape[1] - 16
    code = widen(ref[at, n:, :])[:1]
    return widen(ref[at, :n, :]) * scale_of(code)


def put_wide(ref, at, x):
    row = lax.broadcasted_iota(jnp.int32, (16, 128), 0) % 4
    codes = jnp.zeros((16, 128), jnp.float32)
    for g in range(4):
        part = x[:, g * 128 : (g + 1) * 128]
        code = scale_code(part)
        ref[at, g * 16 : (g + 1) * 16, :] = encode(part, code)
        codes = jnp.where(row == g, jnp.broadcast_to(code, (16, 128)), codes)
    ref[at, 64:, :] = codes.astype(jnp.int32).astype(jnp.int16)


def get_wide(ref, at):
    scales = scale_of(widen(ref[at, 64:, :]))
    return [widen(ref[at, g * 16 : (g + 1) * 16, :]) * scales[g : g + 1] for g in range(4)]


def split(x):
    hi = x.astype(jnp.bfloat16)
    return hi, (x - hi.astype(jnp.float32)).astype(jnp.bfloat16)


def dot3(a, b):
    (ah, al), (bh, bl) = a, b
    dot = lambda u, v: jnp.dot(u, v, preferred_element_type=jnp.float32)
    return dot(ah, bh) + (dot(ah, bl) + dot(al, bh))


def kernel(
    pattern_in, lower, upper, ancestor, linv, uinv, out,
    pattern, a_ref, b_ref, bp_ref, anc, lin, uin, parts, peer,
    ms, mr, ns, nr, zs, zr,
    pp, px, ps, pr, ags, agr, agp, fp, wh, wl,
    in_sem, b_sem, d_ss, d_rs, m_ss, m_rs, n_ss, n_rs, z_ss, z_rs,
    px_sem, p_ss, p_rs, ag_ss, ag_rs, agp_sem, corner, token,
):
    y, z, col = (lax.axis_index(k) for k in ("layer", "row", "col"))
    x, c = col >> 1, col & 1
    other = 1 - c
    inner = z > 0

    def dev(dy, dx):
        return ((y + dy) & 3, z, ((x + dx) & 3) * 2 + c)

    near_a = {d: dev(c * d, other * d) for d in (1, -1)}
    near_b = {d: dev(other * d, c * d) for d in (1, 2, 3)}

    twin = (y, z, x * 2 + other)

    up, down = (y, (z + 1) & (NZ - 1), col), (y, (z - 1) & (NZ - 1), col)

    loads = [
        pltpu.make_async_copy(lower.at[0], a_ref, in_sem.at[0]),
        pltpu.make_async_copy(ancestor, anc, in_sem.at[1]),
        pltpu.make_async_copy(uinv, uin, in_sem.at[2]),
        pltpu.make_async_copy(linv, lin, in_sem.at[3]),
        pltpu.make_async_copy(pattern_in, pattern, in_sem.at[4]),
    ]
    b_loads = []
    for k, (dy, dx) in enumerate(ORDER):
        first = ((y + dy) & 3) * 1024 + ((x + dx) & 3) * 256
        b_loads.append(
            pltpu.make_async_copy(
                upper.at[0, :, pl.ds(pl.multiple_of(first, 256), 256)], b_ref.at[k], b_sem.at[k]
            )
        )
    bp_loads = [
        pltpu.make_async_copy(upper.at[0, :, q * 256 : (q + 1) * 256], bp_ref.at[q], b_sem.at[16 + q])
        for q in range(2)
    ]
    barrier = pltpu.get_barrier_semaphore()
    partners = [twin] + [dev(0, d) for d in (1, 2, 3)] + [dev(d, 0) for d in (1, 2, 3)]
    partners += [up, down]
    for partner in partners:
        pl.semaphore_signal(barrier, inc=1, device_id=partner, device_id_type=MESH)

    loads[0].start()
    loads[4].start()

    @pl.when(inner)
    def _():
        for cp in bp_loads:
            cp.start()

    for cp in b_loads[:3]:
        cp.start()
    loads[1].start()

    loads[4].wait()
    loads[0].wait()
    for cp in b_loads[3:9]:
        cp.start()
    for rb in range(ROWS // BLK):
        for kb in range(KS // 512):
            node = (col * KS + kb * 512) // SNW
            keep = pattern[node, 0, z * (ROWS // BLK) + rb].astype(jnp.float32)
            at = (slice(rb * BLK, (rb + 1) * BLK), slice(kb * 512, (kb + 1) * 512))
            a_ref[at] = (a_ref[at].astype(jnp.float32) * keep).astype(jnp.bfloat16)

    loads[1].wait()

    @pl.when(inner)
    def _():
        for q in range(2):
            bp_loads[q].wait()
        for q in range(2):
            pp[:, q * 256 : (q + 1) * 256] = jnp.dot(
                a_ref[...], bp_ref[q], preferred_element_type=jnp.float32
            )

        @pl.when((y == 0) & (col < 4))
        def _():
            here = pl.ds(pl.multiple_of(col * 128, 128), 128)
            pp[:, here] -= anc[...]


    px_copy = pltpu.make_async_remote_copy(
        src_ref=pp.at[pl.ds(pl.multiple_of(other * HALF, HALF), HALF)],
        dst_ref=px,
        send_sem=px_sem.at[0],
        recv_sem=px_sem.at[1],
        device_id=twin,
        device_id_type=MESH,
    )

    def enter():
        pl.semaphore_wait(barrier, len(partners))

        @pl.when(inner)
        def _():
            px_copy.start()
            for d in (1, 2, 3):
                pl.semaphore_signal(corner, inc=1, device_id=dev(0, d), device_id_type=MESH)

    def pass_token():
        @pl.when((z == 1) | (z == 2) | (z == 3) | (z == 6) | (z == 7))
        def _():
            pl.semaphore_wait(token, 1)

        @pl.when((z >= 1) & (z <= 4))
        def _():
            pl.semaphore_signal(token, inc=1, device_id=down, device_id_type=MESH)

        @pl.when(z >= 5)
        def _():
            pl.semaphore_signal(token, inc=1, device_id=up, device_id_type=MESH)

    def p_copy(i):
        return pltpu.make_async_remote_copy(
            src_ref=ps.at[chip_at(i)],
            dst_ref=pr.at[i],
            send_sem=p_ss.at[i],
            recv_sem=p_rs.at[i],
            device_id=dev(i // 4, i % 4),
            device_id_type=MESH,
        )

    def ag_copy(i):
        return pltpu.make_async_remote_copy(
            src_ref=ags.at[0],
            dst_ref=agr.at[i],
            send_sem=ag_ss.at[i],
            recv_sem=ag_rs.at[i],
            device_id=dev(i // 4, i % 4),
            device_id_type=MESH,
        )

    agp_copy = pltpu.make_async_remote_copy(
        src_ref=agr,
        dst_ref=agp,
        send_sem=agp_sem.at[0],
        recv_sem=agp_sem.at[1],
        device_id=twin,
        device_id_type=MESH,
    )

    def chip_at(i):
        return ((y + i // 4) & 3) * 4 + ((x + i % 4) & 3)

    def chip_from(i):
        return ((y - i // 4) & 3) * 4 + ((x - i % 4) & 3)

    def panel_send():
        @pl.when(inner)
        def _():
            px_copy.wait_recv()
            pl.semaphore_wait(corner, 3)
            mine = pp[pl.ds(pl.multiple_of(c * HALF, HALF), HALF), :] + px[...]
            px[...] = mine
            for j in range(16):
                put_wide(ps, j, mine[j * 16 : (j + 1) * 16])
            for i in range(1, 16):
                p_copy(i).start()

    def panel_sum():
        @pl.when(inner)
        def _():
            for i in range(1, 16):
                p_copy(i).wait_recv()
            total = px[pl.ds(pl.multiple_of(chip_at(0) * 16, 16), 16), :]
            for i in range(1, 16):
                total = total + jnp.concatenate(get_wide(pr, i), axis=1)
            put_wide(ags, 0, -total)
            agr[0] = ags[0]
            for i in range(1, 16):
                ag_copy(i).start()

    def panel_gather():
        @pl.when(inner)
        def _():
            for i in range(1, 16):
                ag_copy(i).wait_recv()
            agp_copy.start()

    def panel_use():
        @pl.when(inner)
        def _():
            def unpack(ref, half):
                for i in range(16):
                    at = pl.multiple_of(half * HALF + chip_from(i) * 16, 16)
                    for g, part in enumerate(get_wide(ref, i)):
                        fp[pl.ds(at, 16), g * 128 : (g + 1) * 128] = part

            unpack(agr, c)
            agp_copy.wait_recv()
            unpack(agp, other)
            loads[2].wait()
            loads[3].wait()
            panel = dot3(split(fp[...]), split(uin[...]))
            fp[...] = panel
            w = dot3(split(panel), split(lin[...]))
            wh[...], wl[...] = split(w)

    def slots(k):
        dy, dx = ORDER[k]
        return dx * 4 + dy, dy * 4 + dx

    def d_copy(k):
        s0, s1 = slots(k)
        s = jnp.where(c == 0, s1, s0)
        return pltpu.make_async_remote_copy(
            src_ref=parts.at[other, s],
            dst_ref=peer.at[s],
            send_sem=d_ss.at[s],
            recv_sem=d_rs.at[s],
            device_id=twin,
            device_id_type=MESH,
        )

    def compute(*ks):
        for k in ks:
            b_loads[k].wait()
        tiles = 2 // len(ks)
        for k in ks:
            s0, s1 = slots(k)
            for t in range(tiles):
                at = slice(t * ROWS // tiles, (t + 1) * ROWS // tiles)
                both = jnp.dot(a_ref[at], b_ref[k], preferred_element_type=jnp.float32)
                parts[0, s0, at] = both[:, :128]
                parts[1, s1, at] = both[:, 128:]

    def step(*ks):
        compute(*ks)
        for k in ks:
            d_copy(k).start()

    here = set()

    def arrive(da, db):
        s = da * 4 + db
        if s not in here:
            here.add(s)
            pltpu.make_async_copy(peer.at[s], peer.at[s], d_rs.at[s]).wait()

    def chip_sum(da, db, at):
        s = da * 4 + db
        return parts[c, s, at, :] + peer[s, at, :]

    def rows(h):
        return slice(h * HALF, (h + 1) * HALF)

    def quarter(h, q):
        return slice(h * HALF + q * QUARTER, h * HALF + (q + 1) * QUARTER)

    def m_at(kind, way, h, db):
        return ((kind * 2 + way) * 2 + h) * 4 + db

    def m_copy(kind, way, h, db):
        at = m_at(kind, way, h, db)
        return pltpu.make_async_remote_copy(
            src_ref=ms.at[at],
            dst_ref=mr.at[at],
            send_sem=m_ss.at[at],
            recv_sem=m_rs.at[at],
            device_id=near_a[1 if way == 0 else -1],
            device_id_type=MESH,
        )

    def m1(h, db):
        return [(0, 0, h, 2, db, 0), (0, 1, h, 2, db, 1)]

    def m2(h, db):
        return [(1, 0, h, 1, db, 1), (1, 1, h, 3, db, 0)]

    def m3(h, db):
        return [(2, 0, h, 1, db, 0), (2, 1, h, 3, db, 1)]

    def send(*groups):
        group = [m for g in groups for m in g]
        for kind, way, h, da, db, q in group:
            arrive(da, db)
            if kind == 2:
                m_copy(0, way, h, db).wait_recv()
        for kind, way, h, da, db, q in group:
            value = chip_sum(da, db, quarter(h, q))
            if kind == 2:
                value = value + get(mr, m_at(0, way, h, db))
            put(ms, m_at(kind, way, h, db), value)
        for kind, way, h, da, db, q in group:
            m_copy(kind, way, h, db).start()

    def n_copy(d, h):
        at = (d - 1) * 2 + h
        return pltpu.make_async_remote_copy(
            src_ref=ns.at[at],
            dst_ref=nr.at[at],
            send_sem=n_ss.at[at],
            recv_sem=n_rs.at[at],
            device_id=near_b[d],
            device_id_type=MESH,
        )

    sources = (((2, 0), (1, 1)), ((1, 0), (2, 1)))

    def first_wait(db, h):
        arrive(0, db)
        for q in range(2):
            for kind, way in sources[q]:
                m_copy(kind, way, h, db).wait_recv()

    def first_sum(db, h):
        sums = []
        for q in range(2):
            total = chip_sum(0, db, quarter(h, q))
            for kind, way in sources[q]:
                total = total + get(mr, m_at(kind, way, h, db))
            sums.append(total)
        return jnp.concatenate(sums, axis=0)

    def n_send(h, *dbs):
        for db in dbs:
            first_wait(db, h)
        for db in dbs:
            put(ns, (db - 1) * 2 + h, first_sum(db, h))
        for db in dbs:
            n_copy(db, h).start()

    compute(0)
    for cp in b_loads[9:]:
        cp.start()
    loads[2].start()
    loads[3].start()
    compute(1, 2)
    compute(3, 4)
    compute(5, 6)
    enter()
    d_copy(0).start()
    d_copy(1).start()
    d_copy(2).start()
    send(m1(0, 2), m1(1, 2))
    for k in range(3, 7):
        d_copy(k).start()
    step(7, 8)
    panel_send()
    send(m1(0, 1), m1(0, 3))
    step(9, 10)
    send(m1(0, 0), m2(0, 2), m1(1, 1))
    pass_token()
    step(11, 12)
    send(m2(0, 1), m2(0, 3), m1(1, 3))
    send(m3(0, 2), m1(1, 0))
    step(13, 14)
    send(m3(0, 1), m2(1, 2))
    step(15)
    send(m3(0, 3))
    send(m3(1, 2), m2(1, 1), m2(1, 3))
    send(m2(0, 0), m3(0, 0))
    panel_sum()
    n_send(0, 2)
    send(m3(1, 1), m3(1, 3), m2(1, 0))
    n_send(0, 1, 3)
    send(m3(1, 0))
    panel_gather()
    n_send(1, 2)
    n_send(1, 1, 3)

    def z_copy(d, h):
        at = d * 2 + h
        return pltpu.make_async_remote_copy(
            src_ref=zs.at[h],
            dst_ref=zr.at[h],
            send_sem=z_ss.at[at],
            recv_sem=z_rs.at[h],
            device_id=(y, d, col),
            device_id_type=MESH,
        )

    def final_sum(h):
        first_wait(0, h)
        for d in (1, 2, 3):
            n_copy(d, h).wait_recv()
        total = first_sum(0, h)
        for d in (1, 2, 3):
            total = total + get(nr, (d - 1) * 2 + h)
        return anc[rows(h), :] - total

    relay = (z == 1) | (z == 3) | (z == 7)
    relay_copy = pltpu.make_async_remote_copy(
        src_ref=zr.at[0],
        dst_ref=zr.at[0],
        send_sem=z_ss.at[0],
        recv_sem=z_rs.at[0],
        device_id=(y, jnp.where(z == 7, 6, z + 1), col),
        device_id_type=MESH,
    )

    @pl.when(relay)
    def _():
        z_copy(0, 0).wait_recv()
        relay_copy.start()

    panel_use()
    for h in range(2):
        out[rows(h), :] = final_sum(h)

        @pl.when(z == 0)
        def _():
            put(zs, h, out[rows(h), :])
            if h == 0:
                pl.semaphore_wait(token, 2)
            for d in FIRST if h == 0 else FAR:
                z_copy(d, h).start()

    in_panel = (y == 0) & (col < 4)

    @pl.when(z == 0)
    def _():
        loads[2].wait()
        loads[3].wait()

        @pl.when(jnp.logical_not(in_panel))
        def _():
            out[...] = dot3(split(lin[...]), split(out[...]))

        for h in range(2):
            for d in FIRST if h == 0 else FAR:
                z_copy(d, h).wait_send()

    @pl.when(inner)
    def _():
        @pl.when(jnp.logical_not(relay))
        def _():
            z_copy(0, 0).wait_recv()

        @pl.when(in_panel)
        def _():
            z_copy(0, 1).wait_recv()
            out[...] = fp[:, pl.ds(pl.multiple_of(col * 128, 128), 128)]

        @pl.when(jnp.logical_not(in_panel))
        def _():
            for h in range(2):
                if h == 1:
                    z_copy(0, 1).wait_recv()
                w = (wh[:, rows(h)], wl[:, rows(h)])
                out[...] -= dot3(w, split(get(zr, h)))

        @pl.when(relay)
        def _():
            relay_copy.wait_send()

        px_copy.wait_send()
        agp_copy.wait_send()

        for i in range(1, 16):
            p_copy(i).wait_send()
            ag_copy(i).wait_send()

    for k in range(16):
        d_copy(k).wait_send()
    for at in range(48):
        m_copy(at // 16, at // 8 % 2, at // 4 % 2, at % 4).wait_send()
    for d in range(1, 4):
        for h in range(2):
            n_copy(d, h).wait_send()


def shards(lower, upper, pattern, ancestor, lower_inverse, upper_inverse):
    f32, bf16, i16 = jnp.float32, jnp.bfloat16, jnp.int16
    vmem, dma = pltpu.VMEM, pltpu.SemaphoreType.DMA
    hbm = pl.BlockSpec(memory_space=pl.ANY)
    msg = HALF + 16
    return pl.pallas_call(
        kernel,
        out_shape=pltpu.VMEM((ROWS, 128), f32),
        in_specs=[hbm] * 6,
        out_specs=pl.BlockSpec(memory_space=pltpu.VMEM),
        scratch_shapes=[
            pltpu.SMEM((6, 1, 32), jnp.int32),
            vmem((ROWS, KS), bf16),
            vmem((16, KS, 256), bf16),
            vmem((2, KS, 256), bf16),
            vmem((ROWS, 128), f32),
            vmem((NB, NB), f32),
            vmem((NB, NB), f32),
            vmem((2, 16, ROWS, 128), f32),
            vmem((16, ROWS, 128), f32),
            vmem((48, QUARTER + 16, 128), i16),
            vmem((48, QUARTER + 16, 128), i16),
            vmem((6, msg, 128), i16),
            vmem((6, msg, 128), i16),
            vmem((2, msg, 128), i16),
            vmem((2, msg, 128), i16),
            vmem((ROWS, NB), f32),
            vmem((HALF, NB), f32),
            vmem((16, 80, 128), i16),
            vmem((16, 80, 128), i16),
            vmem((1, 80, 128), i16),
            vmem((16, 80, 128), i16),
            vmem((16, 80, 128), i16),
            vmem((ROWS, NB), f32),
            vmem((ROWS, NB), bf16),
            vmem((ROWS, NB), bf16),
            dma((5,)),
            dma((18,)),
            dma((16,)),
            dma((16,)),
            dma((48,)),
            dma((48,)),
            dma((6,)),
            dma((6,)),
            dma((16,)),
            dma((2,)),
            dma((2,)),
            dma((16,)),
            dma((16,)),
            dma((16,)),
            dma((16,)),
            dma((2,)),
            pltpu.SemaphoreType.REGULAR,
            pltpu.SemaphoreType.REGULAR,
        ],
        compiler_params=pltpu.CompilerParams(
            collective_id=0, has_side_effects=True, vmem_limit_bytes=56 * 2**20
        ),
    )(jnp.transpose(pattern, (2, 0, 1)), lower, upper, ancestor, lower_inverse, upper_inverse)


def solution(mesh):
    in_specs = (
        P("layer", "row", "col"),
        P("layer", "col", None),
        P("layer", None, None),
        P("row", ("layer", "col")),
        P(),
        P(),
    )
    out_specs = P("row", ("layer", "col"))
    return jax.shard_map(shards, mesh=mesh, in_specs=in_specs, out_specs=out_specs, check_vma=False)
```

```python
import math

import jax
import jax.numpy as jnp
from jax import lax
from jax.experimental import pallas as pl
from jax.experimental.pallas import tpu as pltpu
from jax.sharding import PartitionSpec as P

MESH = pl.DeviceIdType.MESH
SNW = 2048
BLK = 128
NX, NY, NZ = 4, 4, 8
ROWS = 512
HALF = 256
QUARTER = 128
KS = 1536
NB = 512
ORDER = (
    (2, 2),
    (2, 1), (1, 2),
    (2, 3), (3, 2),
    (2, 0), (0, 2),
    (1, 1), (3, 3),
    (1, 3), (3, 1),
    (1, 0), (0, 1),
    (3, 0), (0, 3),
    (0, 0),
)
FIRST = (3, 5, 1, 7)
FAR = (4, 3, 5, 2, 6, 1, 7)
STEP = 16.0 / math.log(2.0)
TOP = 32700.0


def scale_code(x):
    top = jnp.max(jnp.abs(x), axis=0, keepdims=True)
    return jnp.ceil(jnp.log(jnp.maximum(top, 1e-30)) * STEP)


def encode(x, code):
    return jnp.round(x * (jnp.exp(code * (-1.0 / STEP)) * TOP)).astype(jnp.int32).astype(jnp.int16)


def scale_of(code):
    return jnp.exp(code * (1.0 / STEP)) * (1.0 / TOP)


def widen(q):
    return q.astype(jnp.int32).astype(jnp.float32)


def put(ref, at, x):
    n = x.shape[0]
    code = scale_code(x)
    ref[at, :n, :] = encode(x, code)
    ref[at, n:, :] = jnp.broadcast_to(code, (16, x.shape[1])).astype(jnp.int32).astype(jnp.int16)


def get(ref, at):
    n = ref.shape[1] - 16
    code = widen(ref[at, n:, :])[:1]
    return widen(ref[at, :n, :]) * scale_of(code)


def put_wide(ref, at, x):
    row = lax.broadcasted_iota(jnp.int32, (16, 128), 0) % 4
    codes = jnp.zeros((16, 128), jnp.float32)
    for g in range(4):
        part = x[:, g * 128 : (g + 1) * 128]
        code = scale_code(part)
        ref[at, g * 16 : (g + 1) * 16, :] = encode(part, code)
        codes = jnp.where(row == g, jnp.broadcast_to(code, (16, 128)), codes)
    ref[at, 64:, :] = codes.astype(jnp.int32).astype(jnp.int16)


def get_wide(ref, at):
    scales = scale_of(widen(ref[at, 64:, :]))
    return [widen(ref[at, g * 16 : (g + 1) * 16, :]) * scales[g : g + 1] for g in range(4)]


def split(x):
    hi = x.astype(jnp.bfloat16)
    return hi, (x - hi.astype(jnp.float32)).astype(jnp.bfloat16)


def dot3(a, b):
    (ah, al), (bh, bl) = a, b
    dot = lambda u, v: jnp.dot(u, v, preferred_element_type=jnp.float32)
    return dot(ah, bh) + (dot(ah, bl) + dot(al, bh))


def kernel(
    pattern_in, lower, upper, ancestor, linv, uinv, out,
    pattern, a_ref, b_ref, bp_ref, anc, lin, uin, parts, peer,
    ms, mr, ns, nr, zs, zr,
    pp, px, ps, pr, ags, agr, agp, fp, wh, wl,
    in_sem, b_sem, d_ss, d_rs, m_ss, m_rs, n_ss, n_rs, z_ss, z_rs,
    px_sem, p_ss, p_rs, ag_ss, ag_rs, agp_sem, corner, token,
):
    y, z, col = (lax.axis_index(k) for k in ("layer", "row", "col"))
    x, c = col >> 1, col & 1
    other = 1 - c
    inner = z > 0

    def dev(dy, dx):
        return ((y + dy) & 3, z, ((x + dx) & 3) * 2 + c)

    near_a = {d: dev(c * d, other * d) for d in (1, -1)}
    near_b = {d: dev(other * d, c * d) for d in (1, 2, 3)}

    twin = (y, z, x * 2 + other)

    up, down = (y, (z + 1) & (NZ - 1), col), (y, (z - 1) & (NZ - 1), col)

    loads = [
        pltpu.make_async_copy(lower.at[0], a_ref, in_sem.at[0]),
        pltpu.make_async_copy(ancestor, anc, in_sem.at[1]),
        pltpu.make_async_copy(uinv, uin, in_sem.at[2]),
        pltpu.make_async_copy(linv, lin, in_sem.at[3]),
        pltpu.make_async_copy(pattern_in, pattern, in_sem.at[4]),
    ]
    b_loads = []
    for k, (dy, dx) in enumerate(ORDER):
        first = ((y + dy) & 3) * 1024 + ((x + dx) & 3) * 256
        b_loads.append(
            pltpu.make_async_copy(
                upper.at[0, :, pl.ds(pl.multiple_of(first, 256), 256)], b_ref.at[k], b_sem.at[k]
            )
        )
    bp_loads = [
        pltpu.make_async_copy(upper.at[0, :, q * 256 : (q + 1) * 256], bp_ref.at[q], b_sem.at[16 + q])
        for q in range(2)
    ]
    barrier = pltpu.get_barrier_semaphore()
    partners = [twin] + [dev(0, d) for d in (1, 2, 3)] + [dev(d, 0) for d in (1, 2, 3)]
    partners += [up, down]
    for partner in partners:
        pl.semaphore_signal(barrier, inc=1, device_id=partner, device_id_type=MESH)

    loads[0].start()
    loads[4].start()

    @pl.when(inner)
    def _():
        for cp in bp_loads:
            cp.start()

    for cp in b_loads[:3]:
        cp.start()
    loads[1].start()

    loads[4].wait()
    loads[0].wait()
    for cp in b_loads[3:9]:
        cp.start()
    for rb in range(ROWS // BLK):
        for kb in range(KS // 512):
            node = (col * KS + kb * 512) // SNW
            keep = pattern[node, 0, z * (ROWS // BLK) + rb].astype(jnp.float32)
            at = (slice(rb * BLK, (rb + 1) * BLK), slice(kb * 512, (kb + 1) * 512))
            a_ref[at] = (a_ref[at].astype(jnp.float32) * keep).astype(jnp.bfloat16)

    loads[1].wait()

    @pl.when(inner)
    def _():
        for q in range(2):
            bp_loads[q].wait()
        for q in range(2):
            pp[:, q * 256 : (q + 1) * 256] = jnp.dot(
                a_ref[...], bp_ref[q], preferred_element_type=jnp.float32
            )

        @pl.when((y == 0) & (col < 4))
        def _():
            here = pl.ds(pl.multiple_of(col * 128, 128), 128)
            pp[:, here] -= anc[...]


    px_copy = pltpu.make_async_remote_copy(
        src_ref=pp.at[pl.ds(pl.multiple_of(other * HALF, HALF), HALF)],
        dst_ref=px,
        send_sem=px_sem.at[0],
        recv_sem=px_sem.at[1],
        device_id=twin,
        device_id_type=MESH,
    )

    def enter():
        pl.semaphore_wait(barrier, len(partners))

        @pl.when(inner)
        def _():
            px_copy.start()
            for d in (1, 2, 3):
                pl.semaphore_signal(corner, inc=1, device_id=dev(0, d), device_id_type=MESH)

    def pass_token(above, below):
        @pl.when(z == above)
        def _():
            if above < 4:
                pl.semaphore_wait(token, 1)
            pl.semaphore_signal(token, inc=1, device_id=down, device_id_type=MESH)

        @pl.when(z == below)
        def _():
            if below > 5:
                pl.semaphore_wait(token, 1)
            pl.semaphore_signal(token, inc=1, device_id=up, device_id_type=MESH)

    def p_copy(i):
        return pltpu.make_async_remote_copy(
            src_ref=ps.at[chip_at(i)],
            dst_ref=pr.at[i],
            send_sem=p_ss.at[i],
            recv_sem=p_rs.at[i],
            device_id=dev(i // 4, i % 4),
            device_id_type=MESH,
        )

    def ag_copy(i):
        return pltpu.make_async_remote_copy(
            src_ref=ags.at[0],
            dst_ref=agr.at[i],
            send_sem=ag_ss.at[i],
            recv_sem=ag_rs.at[i],
            device_id=dev(i // 4, i % 4),
            device_id_type=MESH,
        )

    agp_copy = pltpu.make_async_remote_copy(
        src_ref=agr,
        dst_ref=agp,
        send_sem=agp_sem.at[0],
        recv_sem=agp_sem.at[1],
        device_id=twin,
        device_id_type=MESH,
    )

    def chip_at(i):
        return ((y + i // 4) & 3) * 4 + ((x + i % 4) & 3)

    def chip_from(i):
        return ((y - i // 4) & 3) * 4 + ((x - i % 4) & 3)

    def panel_send():
        @pl.when(inner)
        def _():
            px_copy.wait_recv()
            pl.semaphore_wait(corner, 3)
            mine = pp[pl.ds(pl.multiple_of(c * HALF, HALF), HALF), :] + px[...]
            px[...] = mine
            for j in range(16):
                put_wide(ps, j, mine[j * 16 : (j + 1) * 16])
            for i in range(1, 16):
                p_copy(i).start()

    def panel_sum():
        @pl.when(inner)
        def _():
            for i in range(1, 16):
                p_copy(i).wait_recv()
            total = px[pl.ds(pl.multiple_of(chip_at(0) * 16, 16), 16), :]
            for i in range(1, 16):
                total = total + jnp.concatenate(get_wide(pr, i), axis=1)
            put_wide(ags, 0, -total)
            agr[0] = ags[0]
            for i in range(1, 16):
                ag_copy(i).start()

    def panel_gather():
        @pl.when(inner)
        def _():
            for i in range(1, 16):
                ag_copy(i).wait_recv()
            agp_copy.start()

    def panel_use():
        @pl.when(inner)
        def _():
            def unpack(ref, half):
                for i in range(16):
                    at = pl.multiple_of(half * HALF + chip_from(i) * 16, 16)
                    for g, part in enumerate(get_wide(ref, i)):
                        fp[pl.ds(at, 16), g * 128 : (g + 1) * 128] = part

            unpack(agr, c)
            agp_copy.wait_recv()
            unpack(agp, other)
            loads[2].wait()
            loads[3].wait()
            panel = dot3(split(fp[...]), split(uin[...]))
            fp[...] = panel
            w = dot3(split(panel), split(lin[...]))
            wh[...], wl[...] = split(w)

    def slots(k):
        dy, dx = ORDER[k]
        return dx * 4 + dy, dy * 4 + dx

    def d_copy(k):
        s0, s1 = slots(k)
        s = jnp.where(c == 0, s1, s0)
        return pltpu.make_async_remote_copy(
            src_ref=parts.at[other, s],
            dst_ref=peer.at[s],
            send_sem=d_ss.at[s],
            recv_sem=d_rs.at[s],
            device_id=twin,
            device_id_type=MESH,
        )

    def compute(*ks):
        for k in ks:
            b_loads[k].wait()
        tiles = 2 // len(ks)
        for k in ks:
            s0, s1 = slots(k)
            for t in range(tiles):
                at = slice(t * ROWS // tiles, (t + 1) * ROWS // tiles)
                both = jnp.dot(a_ref[at], b_ref[k], preferred_element_type=jnp.float32)
                parts[0, s0, at] = both[:, :128]
                parts[1, s1, at] = both[:, 128:]

    def step(*ks):
        compute(*ks)
        for k in ks:
            d_copy(k).start()

    here = set()

    def arrive(da, db):
        s = da * 4 + db
        if s not in here:
            here.add(s)
            pltpu.make_async_copy(peer.at[s], peer.at[s], d_rs.at[s]).wait()

    def chip_sum(da, db, at):
        s = da * 4 + db
        return parts[c, s, at, :] + peer[s, at, :]

    def rows(h):
        return slice(h * HALF, (h + 1) * HALF)

    def quarter(h, q):
        return slice(h * HALF + q * QUARTER, h * HALF + (q + 1) * QUARTER)

    def m_at(kind, way, h, db):
        return ((kind * 2 + way) * 2 + h) * 4 + db

    def m_copy(kind, way, h, db):
        at = m_at(kind, way, h, db)
        return pltpu.make_async_remote_copy(
            src_ref=ms.at[at],
            dst_ref=mr.at[at],
            send_sem=m_ss.at[at],
            recv_sem=m_rs.at[at],
            device_id=near_a[1 if way == 0 else -1],
            device_id_type=MESH,
        )

    def m1(h, db):
        return [(0, 0, h, 2, db, 0), (0, 1, h, 2, db, 1)]

    def m2(h, db):
        return [(1, 0, h, 1, db, 1), (1, 1, h, 3, db, 0)]

    def m3(h, db):
        return [(2, 0, h, 1, db, 0), (2, 1, h, 3, db, 1)]

    def send(*groups):
        group = [m for g in groups for m in g]
        for kind, way, h, da, db, q in group:
            arrive(da, db)
            if kind == 2:
                m_copy(0, way, h, db).wait_recv()
        for kind, way, h, da, db, q in group:
            value = chip_sum(da, db, quarter(h, q))
            if kind == 2:
                value = value + get(mr, m_at(0, way, h, db))
            put(ms, m_at(kind, way, h, db), value)
        for kind, way, h, da, db, q in group:
            m_copy(kind, way, h, db).start()

    def n_copy(d, h):
        at = (d - 1) * 2 + h
        return pltpu.make_async_remote_copy(
            src_ref=ns.at[at],
            dst_ref=nr.at[at],
            send_sem=n_ss.at[at],
            recv_sem=n_rs.at[at],
            device_id=near_b[d],
            device_id_type=MESH,
        )

    sources = (((2, 0), (1, 1)), ((1, 0), (2, 1)))

    def first_wait(db, h):
        arrive(0, db)
        for q in range(2):
            for kind, way in sources[q]:
                m_copy(kind, way, h, db).wait_recv()

    def first_sum(db, h):
        sums = []
        for q in range(2):
            total = chip_sum(0, db, quarter(h, q))
            for kind, way in sources[q]:
                total = total + get(mr, m_at(kind, way, h, db))
            sums.append(total)
        return jnp.concatenate(sums, axis=0)

    def n_send(h, *dbs):
        for db in dbs:
            first_wait(db, h)
        for db in dbs:
            put(ns, (db - 1) * 2 + h, first_sum(db, h))
        for db in dbs:
            n_copy(db, h).start()

    compute(0)
    for cp in b_loads[9:]:
        cp.start()
    loads[2].start()
    loads[3].start()
    compute(1, 2)
    compute(3, 4)
    compute(5, 6)
    enter()
    d_copy(0).start()
    pass_token(4, 5)
    d_copy(1).start()
    d_copy(2).start()
    send(m1(0, 2), m1(1, 2))
    for k in range(3, 7):
        d_copy(k).start()
    step(7, 8)
    panel_send()
    send(m1(0, 1), m1(0, 3))
    step(9, 10)
    send(m1(0, 0), m2(0, 2), m1(1, 1))
    pass_token(3, 6)
    step(11, 12)
    send(m2(0, 1), m2(0, 3), m1(1, 3))
    send(m3(0, 2), m1(1, 0))
    step(13, 14)
    send(m3(0, 1), m2(1, 2))
    pass_token(2, 7)
    step(15)
    send(m3(0, 3))
    send(m3(1, 2), m2(1, 1), m2(1, 3))
    send(m2(0, 0), m3(0, 0))
    panel_sum()
    pass_token(1, -1)
    n_send(0, 2)
    send(m3(1, 1), m3(1, 3), m2(1, 0))
    n_send(0, 1, 3)
    send(m3(1, 0))
    panel_gather()
    n_send(1, 2)
    n_send(1, 1, 3)

    def z_copy(d, h):
        at = d * 2 + h
        return pltpu.make_async_remote_copy(
            src_ref=zs.at[h],
            dst_ref=zr.at[h],
            send_sem=z_ss.at[at],
            recv_sem=z_rs.at[h],
            device_id=(y, d, col),
            device_id_type=MESH,
        )

    def final_sum(h):
        first_wait(0, h)
        for d in (1, 2, 3):
            n_copy(d, h).wait_recv()
        total = first_sum(0, h)
        for d in (1, 2, 3):
            total = total + get(nr, (d - 1) * 2 + h)
        return anc[rows(h), :] - total

    relay = (z == 1) | (z == 3) | (z == 7)
    relay_copy = pltpu.make_async_remote_copy(
        src_ref=zr.at[0],
        dst_ref=zr.at[0],
        send_sem=z_ss.at[0],
        recv_sem=z_rs.at[0],
        device_id=(y, jnp.where(z == 7, 6, z + 1), col),
        device_id_type=MESH,
    )

    @pl.when(relay)
    def _():
        z_copy(0, 0).wait_recv()
        relay_copy.start()

    panel_use()
    for h in range(2):
        out[rows(h), :] = final_sum(h)

        @pl.when(z == 0)
        def _():
            put(zs, h, out[rows(h), :])
            if h == 0:
                pl.semaphore_wait(token, 2)
            for d in FIRST if h == 0 else FAR:
                z_copy(d, h).start()

    in_panel = (y == 0) & (col < 4)

    @pl.when(z == 0)
    def _():
        loads[2].wait()
        loads[3].wait()

        @pl.when(jnp.logical_not(in_panel))
        def _():
            out[...] = dot3(split(lin[...]), split(out[...]))

        for h in range(2):
            for d in FIRST if h == 0 else FAR:
                z_copy(d, h).wait_send()

    @pl.when(inner)
    def _():
        @pl.when(jnp.logical_not(relay))
        def _():
            z_copy(0, 0).wait_recv()

        @pl.when(in_panel)
        def _():
            z_copy(0, 1).wait_recv()
            out[...] = fp[:, pl.ds(pl.multiple_of(col * 128, 128), 128)]

        @pl.when(jnp.logical_not(in_panel))
        def _():
            for h in range(2):
                if h == 1:
                    z_copy(0, 1).wait_recv()
                w = (wh[:, rows(h)], wl[:, rows(h)])
                out[...] -= dot3(w, split(get(zr, h)))

        @pl.when(relay)
        def _():
            relay_copy.wait_send()

        px_copy.wait_send()
        agp_copy.wait_send()

        for i in range(1, 16):
            p_copy(i).wait_send()
            ag_copy(i).wait_send()

    for k in range(16):
        d_copy(k).wait_send()
    for at in range(48):
        m_copy(at // 16, at // 8 % 2, at // 4 % 2, at % 4).wait_send()
    for d in range(1, 4):
        for h in range(2):
            n_copy(d, h).wait_send()


def shards(lower, upper, pattern, ancestor, lower_inverse, upper_inverse):
    f32, bf16, i16 = jnp.float32, jnp.bfloat16, jnp.int16
    vmem, dma = pltpu.VMEM, pltpu.SemaphoreType.DMA
    hbm = pl.BlockSpec(memory_space=pl.ANY)
    msg = HALF + 16
    return pl.pallas_call(
        kernel,
        out_shape=pltpu.VMEM((ROWS, 128), f32),
        in_specs=[hbm] * 6,
        out_specs=pl.BlockSpec(memory_space=pltpu.VMEM),
        scratch_shapes=[
            pltpu.SMEM((6, 1, 32), jnp.int32),
            vmem((ROWS, KS), bf16),
            vmem((16, KS, 256), bf16),
            vmem((2, KS, 256), bf16),
            vmem((ROWS, 128), f32),
            vmem((NB, NB), f32),
            vmem((NB, NB), f32),
            vmem((2, 16, ROWS, 128), f32),
            vmem((16, ROWS, 128), f32),
            vmem((48, QUARTER + 16, 128), i16),
            vmem((48, QUARTER + 16, 128), i16),
            vmem((6, msg, 128), i16),
            vmem((6, msg, 128), i16),
            vmem((2, msg, 128), i16),
            vmem((2, msg, 128), i16),
            vmem((ROWS, NB), f32),
            vmem((HALF, NB), f32),
            vmem((16, 80, 128), i16),
            vmem((16, 80, 128), i16),
            vmem((1, 80, 128), i16),
            vmem((16, 80, 128), i16),
            vmem((16, 80, 128), i16),
            vmem((ROWS, NB), f32),
            vmem((ROWS, NB), bf16),
            vmem((ROWS, NB), bf16),
            dma((5,)),
            dma((18,)),
            dma((16,)),
            dma((16,)),
            dma((48,)),
            dma((48,)),
            dma((6,)),
            dma((6,)),
            dma((16,)),
            dma((2,)),
            dma((2,)),
            dma((16,)),
            dma((16,)),
            dma((16,)),
            dma((16,)),
            dma((2,)),
            pltpu.SemaphoreType.REGULAR,
            pltpu.SemaphoreType.REGULAR,
        ],
        compiler_params=pltpu.CompilerParams(
            collective_id=0, has_side_effects=True, vmem_limit_bytes=56 * 2**20
        ),
    )(jnp.transpose(pattern, (2, 0, 1)), lower, upper, ancestor, lower_inverse, upper_inverse)


def solution(mesh):
    in_specs = (
        P("layer", "row", "col"),
        P("layer", "col", None),
        P("layer", None, None),
        P("row", ("layer", "col")),
        P(),
        P(),
    )
    out_specs = P("row", ("layer", "col"))
    return jax.shard_map(shards, mesh=mesh, in_specs=in_specs, out_specs=out_specs, check_vma=False)
```

```python
import math

import jax
import jax.numpy as jnp
from jax import lax
from jax.experimental import pallas as pl
from jax.experimental.pallas import tpu as pltpu
from jax.sharding import PartitionSpec as P

MESH = pl.DeviceIdType.MESH
SNW = 2048
BLK = 128
NX, NY, NZ = 4, 4, 8
ROWS = 512
HALF = 256
QUARTER = 128
KS = 1536
NB = 512
ORDER = (
    (2, 2),
    (2, 1), (1, 2),
    (2, 3), (3, 2),
    (2, 0), (0, 2),
    (1, 1), (3, 3),
    (1, 3), (3, 1),
    (1, 0), (0, 1),
    (3, 0), (0, 3),
    (0, 0),
)
FIRST = (3, 5, 1, 7)
FAR = (4, 3, 5, 2, 6, 1, 7)
STEP = 16.0 / math.log(2.0)
TOP = 32700.0


def scale_code(x):
    top = jnp.max(jnp.abs(x), axis=0, keepdims=True)
    return jnp.ceil(jnp.log(jnp.maximum(top, 1e-30)) * STEP)


def encode(x, code):
    return jnp.round(x * (jnp.exp(code * (-1.0 / STEP)) * TOP)).astype(jnp.int32).astype(jnp.int16)


def scale_of(code):
    return jnp.exp(code * (1.0 / STEP)) * (1.0 / TOP)


def widen(q):
    return q.astype(jnp.int32).astype(jnp.float32)


def put(ref, at, x):
    n = x.shape[0]
    code = scale_code(x)
    ref[at, :n, :] = encode(x, code)
    ref[at, n:, :] = jnp.broadcast_to(code, (16, x.shape[1])).astype(jnp.int32).astype(jnp.int16)


def get(ref, at):
    n = ref.shape[1] - 16
    code = widen(ref[at, n:, :])[:1]
    return widen(ref[at, :n, :]) * scale_of(code)


def put_wide(ref, at, x):
    row = lax.broadcasted_iota(jnp.int32, (16, 128), 0) % 4
    codes = jnp.zeros((16, 128), jnp.float32)
    for g in range(4):
        part = x[:, g * 128 : (g + 1) * 128]
        code = scale_code(part)
        ref[at, g * 16 : (g + 1) * 16, :] = encode(part, code)
        codes = jnp.where(row == g, jnp.broadcast_to(code, (16, 128)), codes)
    ref[at, 64:, :] = codes.astype(jnp.int32).astype(jnp.int16)


def get_wide(ref, at):
    scales = scale_of(widen(ref[at, 64:, :]))
    return [widen(ref[at, g * 16 : (g + 1) * 16, :]) * scales[g : g + 1] for g in range(4)]


def split(x):
    hi = x.astype(jnp.bfloat16)
    return hi, (x - hi.astype(jnp.float32)).astype(jnp.bfloat16)


def dot3(a, b):
    (ah, al), (bh, bl) = a, b
    dot = lambda u, v: jnp.dot(u, v, preferred_element_type=jnp.float32)
    return dot(ah, bh) + (dot(ah, bl) + dot(al, bh))


def kernel(
    pattern_in, lower, upper, ancestor, linv, uinv, out,
    pattern, a_ref, b_ref, bp_ref, anc, lin, uin, parts, peer,
    ms, mr, ns, nr, zs, zr,
    pp, px, ps, pr, agr, agp, fp, wh, wl,
    in_sem, b_sem, d_ss, d_rs, m_ss, m_rs, n_ss, n_rs, z_ss, z_rs,
    px_sem, p_ss, p_rs, agp_sem, token,
):
    y, z, col = (lax.axis_index(k) for k in ("layer", "row", "col"))
    x, c = col >> 1, col & 1
    other = 1 - c
    inner = z > 0

    def dev(dy, dx):
        return ((y + dy) & 3, z, ((x + dx) & 3) * 2 + c)

    near_a = {d: dev(c * d, other * d) for d in (1, -1)}
    near_b = {d: dev(other * d, c * d) for d in (1, 2, 3)}

    twin = (y, z, x * 2 + other)

    up, down = (y, (z + 1) & (NZ - 1), col), (y, (z - 1) & (NZ - 1), col)

    loads = [
        pltpu.make_async_copy(lower.at[0], a_ref, in_sem.at[0]),
        pltpu.make_async_copy(ancestor, anc, in_sem.at[1]),
        pltpu.make_async_copy(uinv, uin, in_sem.at[2]),
        pltpu.make_async_copy(linv, lin, in_sem.at[3]),
        pltpu.make_async_copy(pattern_in, pattern, in_sem.at[4]),
    ]
    b_loads = []
    for k, (dy, dx) in enumerate(ORDER):
        first = ((y + dy) & 3) * 1024 + ((x + dx) & 3) * 256
        b_loads.append(
            pltpu.make_async_copy(
                upper.at[0, :, pl.ds(pl.multiple_of(first, 256), 256)], b_ref.at[k], b_sem.at[k]
            )
        )
    bp_loads = [
        pltpu.make_async_copy(upper.at[0, :, q * 256 : (q + 1) * 256], bp_ref.at[q], b_sem.at[16 + q])
        for q in range(2)
    ]
    barrier = pltpu.get_barrier_semaphore()
    partners = [twin] + [dev(0, d) for d in (1, 2, 3)] + [dev(d, 0) for d in (1, 2, 3)]
    partners += [up, down]
    for partner in partners:
        pl.semaphore_signal(barrier, inc=1, device_id=partner, device_id_type=MESH)

    loads[0].start()
    loads[4].start()

    @pl.when(inner)
    def _():
        for cp in bp_loads:
            cp.start()

    for cp in b_loads[:3]:
        cp.start()
    loads[1].start()

    loads[4].wait()
    loads[0].wait()
    for cp in b_loads[3:9]:
        cp.start()
    for rb in range(ROWS // BLK):
        for kb in range(KS // 512):
            node = (col * KS + kb * 512) // SNW
            keep = pattern[node, 0, z * (ROWS // BLK) + rb].astype(jnp.float32)
            at = (slice(rb * BLK, (rb + 1) * BLK), slice(kb * 512, (kb + 1) * 512))
            a_ref[at] = (a_ref[at].astype(jnp.float32) * keep).astype(jnp.bfloat16)

    loads[1].wait()

    @pl.when(inner)
    def _():
        for q in range(2):
            bp_loads[q].wait()
        for q in range(2):
            pp[:, q * 256 : (q + 1) * 256] = jnp.dot(
                a_ref[...], bp_ref[q], preferred_element_type=jnp.float32
            )

        @pl.when((y == 0) & (col < 4))
        def _():
            here = pl.ds(pl.multiple_of(col * 128, 128), 128)
            pp[:, here] -= anc[...]


    px_copy = pltpu.make_async_remote_copy(
        src_ref=pp.at[pl.ds(pl.multiple_of(other * HALF, HALF), HALF)],
        dst_ref=px,
        send_sem=px_sem.at[0],
        recv_sem=px_sem.at[1],
        device_id=twin,
        device_id_type=MESH,
    )

    def enter():
        pl.semaphore_wait(barrier, len(partners))

        @pl.when(inner)
        def _():
            px_copy.start()

    def pass_token(above, below):
        @pl.when(z == above)
        def _():
            if above < 4:
                pl.semaphore_wait(token, 1)
            pl.semaphore_signal(token, inc=1, device_id=down, device_id_type=MESH)

        @pl.when(z == below)
        def _():
            if below > 5:
                pl.semaphore_wait(token, 1)
            pl.semaphore_signal(token, inc=1, device_id=up, device_id_type=MESH)

    far_a = {d: dev(c * d, other * d) for d in (1, 2, 3)}
    ONE, TWO, BACK_TWO, BACK_ONE = range(4)

    def p_copy(stage, d):
        src, dst, partner = {
            ONE: (ps.at[pl.ds(d * 4, 4)], pr.at[pl.ds(d * 4, 4)], far_a[d]),
            TWO: (ps.at[d], pr.at[d], near_b[d]),
            BACK_TWO: (agr.at[0], agr.at[d], near_b[d]),
            BACK_ONE: (agr.at[pl.ds(0, 4)], agr.at[pl.ds(d * 4, 4)], far_a[d]),
        }[stage]
        at = stage * 3 + d - 1
        return pltpu.make_async_remote_copy(
            src_ref=src,
            dst_ref=dst,
            send_sem=p_ss.at[at],
            recv_sem=p_rs.at[at],
            device_id=partner,
            device_id_type=MESH,
        )

    agp_copy = pltpu.make_async_remote_copy(
        src_ref=agr,
        dst_ref=agp,
        send_sem=agp_sem.at[0],
        recv_sem=agp_sem.at[1],
        device_id=twin,
        device_id_type=MESH,
    )

    def chip_at(da, db, core):
        dy, dx = core * da + (1 - core) * db, core * db + (1 - core) * da
        return ((y + dy) & 3) * 4 + ((x + dx) & 3)

    def panel_slice(da, db):
        return px[pl.ds(pl.multiple_of(chip_at(da, db, c) * 16, 16), 16), :]

    def panel_one():
        @pl.when(inner)
        def _():
            px_copy.wait_recv()
            px[...] += pp[pl.ds(pl.multiple_of(c * HALF, HALF), HALF), :]
            for d in (2, 1, 3):
                for db in range(4):
                    put_wide(ps, d * 4 + db, panel_slice(d, db))
            for d in (2, 1, 3):
                p_copy(ONE, d).start()

    def panel_two():
        @pl.when(inner)
        def _():
            for d in (1, 2, 3):
                p_copy(ONE, d).wait_recv()
            for db in range(4):
                total = panel_slice(0, db)
                for d in (1, 2, 3):
                    total = total + jnp.concatenate(get_wide(pr, d * 4 + db), axis=1)
                if db == 0:
                    fp[:16] = total
                else:
                    put_wide(ps, db, total)
            for d in (2, 1, 3):
                p_copy(TWO, d).start()

    def panel_three():
        @pl.when(inner)
        def _():
            for d in (1, 2, 3):
                p_copy(TWO, d).wait_recv()
            total = fp[:16]
            for d in (1, 2, 3):
                total = total + jnp.concatenate(get_wide(pr, d), axis=1)
            put_wide(agr, 0, -total)
            for d in (2, 1, 3):
                p_copy(BACK_TWO, d).start()

    def panel_four():
        @pl.when(inner)
        def _():
            for d in (1, 2, 3):
                p_copy(BACK_TWO, d).wait_recv()
            for d in (2, 1, 3):
                p_copy(BACK_ONE, d).start()

    def panel_gather():
        @pl.when(inner)
        def _():
            for d in (1, 2, 3):
                p_copy(BACK_ONE, d).wait_recv()
            agp_copy.start()

    def panel_use():
        @pl.when(inner)
        def _():
            def unpack(ref, core):
                for s in range(16):
                    at = pl.multiple_of(core * HALF + chip_at(-(s // 4), -(s % 4), core) * 16, 16)
                    for g, part in enumerate(get_wide(ref, s)):
                        fp[pl.ds(at, 16), g * 128 : (g + 1) * 128] = part

            unpack(agr, c)
            agp_copy.wait_recv()
            unpack(agp, other)
            loads[2].wait()
            loads[3].wait()
            panel = dot3(split(fp[...]), split(uin[...]))
            fp[...] = panel
            w = dot3(split(panel), split(lin[...]))
            wh[...], wl[...] = split(w)

    def slots(k):
        dy, dx = ORDER[k]
        return dx * 4 + dy, dy * 4 + dx

    def d_copy(k):
        s0, s1 = slots(k)
        s = jnp.where(c == 0, s1, s0)
        return pltpu.make_async_remote_copy(
            src_ref=parts.at[other, s],
            dst_ref=peer.at[s],
            send_sem=d_ss.at[s],
            recv_sem=d_rs.at[s],
            device_id=twin,
            device_id_type=MESH,
        )

    def compute(*ks):
        for k in ks:
            b_loads[k].wait()
        tiles = 2 // len(ks)
        for k in ks:
            s0, s1 = slots(k)
            for t in range(tiles):
                at = slice(t * ROWS // tiles, (t + 1) * ROWS // tiles)
                both = jnp.dot(a_ref[at], b_ref[k], preferred_element_type=jnp.float32)
                parts[0, s0, at] = both[:, :128]
                parts[1, s1, at] = both[:, 128:]

    def step(*ks):
        compute(*ks)
        for k in ks:
            d_copy(k).start()

    here = set()

    def arrive(da, db):
        s = da * 4 + db
        if s not in here:
            here.add(s)
            pltpu.make_async_copy(peer.at[s], peer.at[s], d_rs.at[s]).wait()

    def chip_sum(da, db, at):
        s = da * 4 + db
        return parts[c, s, at, :] + peer[s, at, :]

    def rows(h):
        return slice(h * HALF, (h + 1) * HALF)

    def quarter(h, q):
        return slice(h * HALF + q * QUARTER, h * HALF + (q + 1) * QUARTER)

    def m_at(kind, way, h, db):
        return ((kind * 2 + way) * 2 + h) * 4 + db

    def m_copy(kind, way, h, db):
        at = m_at(kind, way, h, db)
        return pltpu.make_async_remote_copy(
            src_ref=ms.at[at],
            dst_ref=mr.at[at],
            send_sem=m_ss.at[at],
            recv_sem=m_rs.at[at],
            device_id=near_a[1 if way == 0 else -1],
            device_id_type=MESH,
        )

    def m1(h, db):
        return [(0, 0, h, 2, db, 0), (0, 1, h, 2, db, 1)]

    def m2(h, db):
        return [(1, 0, h, 1, db, 1), (1, 1, h, 3, db, 0)]

    def m3(h, db):
        return [(2, 0, h, 1, db, 0), (2, 1, h, 3, db, 1)]

    def send(*groups):
        group = [m for g in groups for m in g]
        for kind, way, h, da, db, q in group:
            arrive(da, db)
            if kind == 2:
                m_copy(0, way, h, db).wait_recv()
        for kind, way, h, da, db, q in group:
            value = chip_sum(da, db, quarter(h, q))
            if kind == 2:
                value = value + get(mr, m_at(0, way, h, db))
            put(ms, m_at(kind, way, h, db), value)
        for kind, way, h, da, db, q in group:
            m_copy(kind, way, h, db).start()

    def n_copy(d, h):
        at = (d - 1) * 2 + h
        return pltpu.make_async_remote_copy(
            src_ref=ns.at[at],
            dst_ref=nr.at[at],
            send_sem=n_ss.at[at],
            recv_sem=n_rs.at[at],
            device_id=near_b[d],
            device_id_type=MESH,
        )

    sources = (((2, 0), (1, 1)), ((1, 0), (2, 1)))

    def first_wait(db, h):
        arrive(0, db)
        for q in range(2):
            for kind, way in sources[q]:
                m_copy(kind, way, h, db).wait_recv()

    def first_sum(db, h):
        sums = []
        for q in range(2):
            total = chip_sum(0, db, quarter(h, q))
            for kind, way in sources[q]:
                total = total + get(mr, m_at(kind, way, h, db))
            sums.append(total)
        return jnp.concatenate(sums, axis=0)

    def n_send(h, *dbs):
        for db in dbs:
            first_wait(db, h)
        for db in dbs:
            put(ns, (db - 1) * 2 + h, first_sum(db, h))
        for db in dbs:
            n_copy(db, h).start()

    compute(0)
    for cp in b_loads[9:]:
        cp.start()
    loads[2].start()
    loads[3].start()
    compute(1, 2)
    compute(3, 4)
    compute(5, 6)
    enter()
    d_copy(0).start()
    pass_token(4, 5)
    d_copy(1).start()
    d_copy(2).start()
    send(m1(0, 2), m1(1, 2))
    for k in range(3, 7):
        d_copy(k).start()
    panel_one()
    step(7, 8)
    send(m1(0, 1), m1(0, 3))
    step(9, 10)
    send(m1(0, 0), m2(0, 2), m1(1, 1))
    pass_token(3, 6)
    step(11, 12)
    send(m2(0, 1), m2(0, 3), m1(1, 3))
    panel_two()
    send(m3(0, 2), m1(1, 0))
    step(13, 14)
    send(m3(0, 1), m2(1, 2))
    pass_token(2, 7)
    step(15)
    panel_three()
    send(m3(0, 3))
    send(m3(1, 2), m2(1, 1), m2(1, 3))
    send(m2(0, 0), m3(0, 0))
    panel_four()
    pass_token(1, -1)
    n_send(0, 2)
    send(m3(1, 1), m3(1, 3), m2(1, 0))
    n_send(0, 1, 3)
    send(m3(1, 0))
    panel_gather()
    n_send(1, 2)
    n_send(1, 1, 3)

    def z_copy(d, h):
        at = d * 2 + h
        return pltpu.make_async_remote_copy(
            src_ref=zs.at[h],
            dst_ref=zr.at[h],
            send_sem=z_ss.at[at],
            recv_sem=z_rs.at[h],
            device_id=(y, d, col),
            device_id_type=MESH,
        )

    def final_sum(h):
        first_wait(0, h)
        for d in (1, 2, 3):
            n_copy(d, h).wait_recv()
        total = first_sum(0, h)
        for d in (1, 2, 3):
            total = total + get(nr, (d - 1) * 2 + h)
        return anc[rows(h), :] - total

    relay = (z == 1) | (z == 3) | (z == 7)
    relay_copy = pltpu.make_async_remote_copy(
        src_ref=zr.at[0],
        dst_ref=zr.at[0],
        send_sem=z_ss.at[0],
        recv_sem=z_rs.at[0],
        device_id=(y, jnp.where(z == 7, 6, z + 1), col),
        device_id_type=MESH,
    )

    @pl.when(relay)
    def _():
        z_copy(0, 0).wait_recv()
        relay_copy.start()

    panel_use()
    for h in range(2):
        out[rows(h), :] = final_sum(h)

        @pl.when(z == 0)
        def _():
            put(zs, h, out[rows(h), :])
            if h == 0:
                pl.semaphore_wait(token, 2)
            for d in FIRST if h == 0 else FAR:
                z_copy(d, h).start()

    in_panel = (y == 0) & (col < 4)

    @pl.when(z == 0)
    def _():
        loads[2].wait()
        loads[3].wait()

        @pl.when(jnp.logical_not(in_panel))
        def _():
            out[...] = dot3(split(lin[...]), split(out[...]))

        for h in range(2):
            for d in FIRST if h == 0 else FAR:
                z_copy(d, h).wait_send()

    @pl.when(inner)
    def _():
        @pl.when(jnp.logical_not(relay))
        def _():
            z_copy(0, 0).wait_recv()

        @pl.when(in_panel)
        def _():
            z_copy(0, 1).wait_recv()
            out[...] = fp[:, pl.ds(pl.multiple_of(col * 128, 128), 128)]

        @pl.when(jnp.logical_not(in_panel))
        def _():
            for h in range(2):
                if h == 1:
                    z_copy(0, 1).wait_recv()
                w = (wh[:, rows(h)], wl[:, rows(h)])
                out[...] -= dot3(w, split(get(zr, h)))

        @pl.when(relay)
        def _():
            relay_copy.wait_send()

        px_copy.wait_send()
        agp_copy.wait_send()

        for stage in range(4):
            for d in (1, 2, 3):
                p_copy(stage, d).wait_send()

    for k in range(16):
        d_copy(k).wait_send()
    for at in range(48):
        m_copy(at // 16, at // 8 % 2, at // 4 % 2, at % 4).wait_send()
    for d in range(1, 4):
        for h in range(2):
            n_copy(d, h).wait_send()


def shards(lower, upper, pattern, ancestor, lower_inverse, upper_inverse):
    f32, bf16, i16 = jnp.float32, jnp.bfloat16, jnp.int16
    vmem, dma = pltpu.VMEM, pltpu.SemaphoreType.DMA
    hbm = pl.BlockSpec(memory_space=pl.ANY)
    msg = HALF + 16
    return pl.pallas_call(
        kernel,
        out_shape=pltpu.VMEM((ROWS, 128), f32),
        in_specs=[hbm] * 6,
        out_specs=pl.BlockSpec(memory_space=pltpu.VMEM),
        scratch_shapes=[
            pltpu.SMEM((6, 1, 32), jnp.int32),
            vmem((ROWS, KS), bf16),
            vmem((16, KS, 256), bf16),
            vmem((2, KS, 256), bf16),
            vmem((ROWS, 128), f32),
            vmem((NB, NB), f32),
            vmem((NB, NB), f32),
            vmem((2, 16, ROWS, 128), f32),
            vmem((16, ROWS, 128), f32),
            vmem((48, QUARTER + 16, 128), i16),
            vmem((48, QUARTER + 16, 128), i16),
            vmem((6, msg, 128), i16),
            vmem((6, msg, 128), i16),
            vmem((2, msg, 128), i16),
            vmem((2, msg, 128), i16),
            vmem((ROWS, NB), f32),
            vmem((HALF, NB), f32),
            vmem((16, 80, 128), i16),
            vmem((16, 80, 128), i16),
            vmem((16, 80, 128), i16),
            vmem((16, 80, 128), i16),
            vmem((ROWS, NB), f32),
            vmem((ROWS, NB), bf16),
            vmem((ROWS, NB), bf16),
            dma((5,)),
            dma((18,)),
            dma((16,)),
            dma((16,)),
            dma((48,)),
            dma((48,)),
            dma((6,)),
            dma((6,)),
            dma((16,)),
            dma((2,)),
            dma((2,)),
            dma((12,)),
            dma((12,)),
            dma((2,)),
            pltpu.SemaphoreType.REGULAR,
        ],
        compiler_params=pltpu.CompilerParams(
            collective_id=0, has_side_effects=True, vmem_limit_bytes=56 * 2**20
        ),
    )(jnp.transpose(pattern, (2, 0, 1)), lower, upper, ancestor, lower_inverse, upper_inverse)


def solution(mesh):
    in_specs = (
        P("layer", "row", "col"),
        P("layer", "col", None),
        P("layer", None, None),
        P("row", ("layer", "col")),
        P(),
        P(),
    )
    out_specs = P("row", ("layer", "col"))
    return jax.shard_map(shards, mesh=mesh, in_specs=in_specs, out_specs=out_specs, check_vma=False)
```

```python
import math

import jax
import jax.numpy as jnp
from jax import lax
from jax.experimental import pallas as pl
from jax.experimental.pallas import tpu as pltpu
from jax.sharding import PartitionSpec as P

MESH = pl.DeviceIdType.MESH
SNW = 2048
BLK = 128
NX, NY, NZ = 4, 4, 8
ROWS = 512
HALF = 256
QUARTER = 128
KS = 1536
NB = 512
ORDER = (
    (2, 2),
    (2, 1), (1, 2),
    (2, 3), (3, 2),
    (2, 0), (0, 2),
    (1, 1), (3, 3),
    (1, 3), (3, 1),
    (1, 0), (0, 1),
    (3, 0), (0, 3),
    (0, 0),
)
FIRST = (3, 5, 1, 7)
FAR = (4, 3, 5, 2, 6, 1, 7)
STEP = 16.0 / math.log(2.0)
TOP = 32700.0


def scale_code(x):
    top = jnp.max(jnp.abs(x), axis=0, keepdims=True)
    return jnp.ceil(jnp.log(jnp.maximum(top, 1e-30)) * STEP)


def encode(x, code):
    return jnp.round(x * (jnp.exp(code * (-1.0 / STEP)) * TOP)).astype(jnp.int32).astype(jnp.int16)


def scale_of(code):
    return jnp.exp(code * (1.0 / STEP)) * (1.0 / TOP)


def widen(q):
    return q.astype(jnp.int32).astype(jnp.float32)


def put(ref, at, x):
    n = x.shape[0]
    code = scale_code(x)
    ref[at, :n, :] = encode(x, code)
    ref[at, n:, :] = jnp.broadcast_to(code, (16, x.shape[1])).astype(jnp.int32).astype(jnp.int16)


def get(ref, at):
    n = ref.shape[1] - 16
    code = widen(ref[at, n:, :])[:1]
    return widen(ref[at, :n, :]) * scale_of(code)


def put_wide(ref, at, x):
    row = lax.broadcasted_iota(jnp.int32, (16, 128), 0) % 4
    codes = jnp.zeros((16, 128), jnp.float32)
    for g in range(4):
        part = x[:, g * 128 : (g + 1) * 128]
        code = scale_code(part)
        ref[at, g * 16 : (g + 1) * 16, :] = encode(part, code)
        codes = jnp.where(row == g, jnp.broadcast_to(code, (16, 128)), codes)
    ref[at, 64:, :] = codes.astype(jnp.int32).astype(jnp.int16)


def get_wide(ref, at):
    scales = scale_of(widen(ref[at, 64:, :]))
    return [widen(ref[at, g * 16 : (g + 1) * 16, :]) * scales[g : g + 1] for g in range(4)]


def split(x):
    hi = x.astype(jnp.bfloat16)
    return hi, (x - hi.astype(jnp.float32)).astype(jnp.bfloat16)


def dot3(a, b):
    (ah, al), (bh, bl) = a, b
    dot = lambda u, v: jnp.dot(u, v, preferred_element_type=jnp.float32)
    return dot(ah, bh) + (dot(ah, bl) + dot(al, bh))


def kernel(
    pattern_in, lower, upper, ancestor, linv, uinv, out,
    pattern, a_ref, b_ref, bp_ref, anc, lin, uin, parts, peer,
    ms, mr, ns, nr, zs, zr,
    pp, px, ps, pr, agr, agp, fp, wh, wl,
    in_sem, b_sem, d_ss, d_rs, m_ss, m_rs, n_ss, n_rs, z_ss, z_rs,
    px_sem, p_ss, p_rs, agp_sem, token,
):
    y, z, col = (lax.axis_index(k) for k in ("layer", "row", "col"))
    x, c = col >> 1, col & 1
    other = 1 - c
    inner = z > 0

    def dev(dy, dx):
        return ((y + dy) & 3, z, ((x + dx) & 3) * 2 + c)

    near_a = {d: dev(c * d, other * d) for d in (1, -1)}
    near_b = {d: dev(other * d, c * d) for d in (1, 2, 3)}

    twin = (y, z, x * 2 + other)

    up, down = (y, (z + 1) & (NZ - 1), col), (y, (z - 1) & (NZ - 1), col)

    loads = [
        pltpu.make_async_copy(lower.at[0], a_ref, in_sem.at[0]),
        pltpu.make_async_copy(ancestor, anc, in_sem.at[1]),
        pltpu.make_async_copy(uinv, uin, in_sem.at[2]),
        pltpu.make_async_copy(linv, lin, in_sem.at[3]),
        pltpu.make_async_copy(pattern_in, pattern, in_sem.at[4]),
    ]
    b_loads = []
    for k, (dy, dx) in enumerate(ORDER):
        first = ((y + dy) & 3) * 1024 + ((x + dx) & 3) * 256
        b_loads.append(
            pltpu.make_async_copy(
                upper.at[0, :, pl.ds(pl.multiple_of(first, 256), 256)], b_ref.at[k], b_sem.at[k]
            )
        )
    bp_loads = [
        pltpu.make_async_copy(upper.at[0, :, q * 256 : (q + 1) * 256], bp_ref.at[q], b_sem.at[16 + q])
        for q in range(2)
    ]
    barrier = pltpu.get_barrier_semaphore()
    partners = [twin] + [dev(0, d) for d in (1, 2, 3)] + [dev(d, 0) for d in (1, 2, 3)]
    partners += [up, down]
    for partner in partners:
        pl.semaphore_signal(barrier, inc=1, device_id=partner, device_id_type=MESH)

    loads[0].start()
    loads[4].start()

    @pl.when(inner)
    def _():
        for cp in bp_loads:
            cp.start()

    for cp in b_loads[:3]:
        cp.start()
    loads[1].start()

    loads[4].wait()
    loads[0].wait()
    for cp in b_loads[3:9]:
        cp.start()
    for rb in range(ROWS // BLK):
        for kb in range(KS // 512):
            node = (col * KS + kb * 512) // SNW
            keep = pattern[node, 0, z * (ROWS // BLK) + rb].astype(jnp.float32)
            at = (slice(rb * BLK, (rb + 1) * BLK), slice(kb * 512, (kb + 1) * 512))
            a_ref[at] = (a_ref[at].astype(jnp.float32) * keep).astype(jnp.bfloat16)

    loads[1].wait()

    @pl.when(inner)
    def _():
        for q in range(2):
            bp_loads[q].wait()
        for q in range(2):
            pp[:, q * 256 : (q + 1) * 256] = jnp.dot(
                a_ref[...], bp_ref[q], preferred_element_type=jnp.float32
            )

        @pl.when((y == 0) & (col < 4))
        def _():
            here = pl.ds(pl.multiple_of(col * 128, 128), 128)
            pp[:, here] -= anc[...]


    px_copy = pltpu.make_async_remote_copy(
        src_ref=pp.at[pl.ds(pl.multiple_of(other * HALF, HALF), HALF)],
        dst_ref=px,
        send_sem=px_sem.at[0],
        recv_sem=px_sem.at[1],
        device_id=twin,
        device_id_type=MESH,
    )

    def enter():
        pl.semaphore_wait(barrier, len(partners))

        @pl.when(inner)
        def _():
            px_copy.start()

    def pass_token(above, below):
        @pl.when(z == above)
        def _():
            if above < 4:
                pl.semaphore_wait(token, 1)
            pl.semaphore_signal(token, inc=1, device_id=down, device_id_type=MESH)

        @pl.when(z == below)
        def _():
            if below > 5:
                pl.semaphore_wait(token, 1)
            pl.semaphore_signal(token, inc=1, device_id=up, device_id_type=MESH)

    far_a = {d: dev(c * d, other * d) for d in (1, 2, 3)}
    ONE, TWO, BACK_TWO, BACK_ONE = range(4)

    def p_copy(stage, d):
        src, dst, partner = {
            ONE: (ps.at[pl.ds(d * 4, 4)], pr.at[pl.ds(d * 4, 4)], far_a[d]),
            TWO: (ps.at[d], pr.at[d], near_b[d]),
            BACK_TWO: (agr.at[0], agr.at[d], near_b[d]),
            BACK_ONE: (agr.at[pl.ds(0, 4)], agr.at[pl.ds(d * 4, 4)], far_a[d]),
        }[stage]
        at = stage * 3 + d - 1
        return pltpu.make_async_remote_copy(
            src_ref=src,
            dst_ref=dst,
            send_sem=p_ss.at[at],
            recv_sem=p_rs.at[at],
            device_id=partner,
            device_id_type=MESH,
        )

    agp_copy = pltpu.make_async_remote_copy(
        src_ref=agr,
        dst_ref=agp,
        send_sem=agp_sem.at[0],
        recv_sem=agp_sem.at[1],
        device_id=twin,
        device_id_type=MESH,
    )

    def chip_at(da, db, core):
        dy, dx = core * da + (1 - core) * db, core * db + (1 - core) * da
        return ((y + dy) & 3) * 4 + ((x + dx) & 3)

    def panel_slice(da, db):
        return px[pl.ds(pl.multiple_of(chip_at(da, db, c) * 16, 16), 16), :]

    def panel_one():
        @pl.when(inner)
        def _():
            px_copy.wait_recv()
            px[...] += pp[pl.ds(pl.multiple_of(c * HALF, HALF), HALF), :]
            for d in (2, 1, 3):
                for db in range(4):
                    put_wide(ps, d * 4 + db, panel_slice(d, db))
            for d in (2, 1, 3):
                p_copy(ONE, d).start()

    def panel_two():
        @pl.when(inner)
        def _():
            for d in (1, 2, 3):
                p_copy(ONE, d).wait_recv()
            for db in range(4):
                total = panel_slice(0, db)
                for d in (1, 2, 3):
                    total = total + jnp.concatenate(get_wide(pr, d * 4 + db), axis=1)
                if db == 0:
                    fp[:16] = total
                else:
                    put_wide(ps, db, total)
            for d in (2, 1, 3):
                p_copy(TWO, d).start()

    def panel_three():
        @pl.when(inner)
        def _():
            for d in (1, 2, 3):
                p_copy(TWO, d).wait_recv()
            total = fp[:16]
            for d in (1, 2, 3):
                total = total + jnp.concatenate(get_wide(pr, d), axis=1)
            put_wide(agr, 0, -total)
            for d in (2, 1, 3):
                p_copy(BACK_TWO, d).start()

    def panel_four():
        @pl.when(inner)
        def _():
            for d in (1, 2, 3):
                p_copy(BACK_TWO, d).wait_recv()
            for d in (2, 1, 3):
                p_copy(BACK_ONE, d).start()

    def panel_gather():
        @pl.when(inner)
        def _():
            for d in (1, 2, 3):
                p_copy(BACK_ONE, d).wait_recv()
            agp_copy.start()

    def panel_use():
        @pl.when(inner)
        def _():
            def unpack(ref, core):
                for s in range(16):
                    at = pl.multiple_of(core * HALF + chip_at(-(s // 4), -(s % 4), core) * 16, 16)
                    for g, part in enumerate(get_wide(ref, s)):
                        fp[pl.ds(at, 16), g * 128 : (g + 1) * 128] = part

            unpack(agr, c)
            agp_copy.wait_recv()
            unpack(agp, other)
            loads[2].wait()
            loads[3].wait()
            panel = dot3(split(fp[...]), split(uin[...]))
            fp[...] = panel
            w = dot3(split(panel), split(lin[...]))
            wh[...], wl[...] = split(w)

    def slots(k):
        dy, dx = ORDER[k]
        return dx * 4 + dy, dy * 4 + dx

    def d_copy(k):
        s0, s1 = slots(k)
        s = jnp.where(c == 0, s1, s0)
        return pltpu.make_async_remote_copy(
            src_ref=parts.at[other, s],
            dst_ref=peer.at[s],
            send_sem=d_ss.at[s],
            recv_sem=d_rs.at[s],
            device_id=twin,
            device_id_type=MESH,
        )

    def compute(*ks):
        for k in ks:
            b_loads[k].wait()
        tiles = 2 // len(ks)
        for k in ks:
            s0, s1 = slots(k)
            for t in range(tiles):
                at = slice(t * ROWS // tiles, (t + 1) * ROWS // tiles)
                both = jnp.dot(a_ref[at], b_ref[k], preferred_element_type=jnp.float32)
                parts[0, s0, at] = both[:, :128]
                parts[1, s1, at] = both[:, 128:]

    def step(*ks):
        compute(*ks)
        for k in ks:
            d_copy(k).start()

    here = set()

    def arrive(da, db):
        s = da * 4 + db
        if s not in here:
            here.add(s)
            pltpu.make_async_copy(peer.at[s], peer.at[s], d_rs.at[s]).wait()

    def chip_sum(da, db, at):
        s = da * 4 + db
        return parts[c, s, at, :] + peer[s, at, :]

    def rows(h):
        return slice(h * HALF, (h + 1) * HALF)

    def quarter(h, q):
        return slice(h * HALF + q * QUARTER, h * HALF + (q + 1) * QUARTER)

    def m_at(kind, way, h, db):
        return ((kind * 2 + way) * 2 + h) * 4 + db

    def m_copy(kind, way, h, db):
        at = m_at(kind, way, h, db)
        return pltpu.make_async_remote_copy(
            src_ref=ms.at[at],
            dst_ref=mr.at[at],
            send_sem=m_ss.at[at],
            recv_sem=m_rs.at[at],
            device_id=near_a[1 if way == 0 else -1],
            device_id_type=MESH,
        )

    def m1(h, db):
        return [(0, 0, h, 2, db, 0), (0, 1, h, 2, db, 1)]

    def m2(h, db):
        return [(1, 0, h, 1, db, 1), (1, 1, h, 3, db, 0)]

    def m3(h, db):
        return [(2, 0, h, 1, db, 0), (2, 1, h, 3, db, 1)]

    def send(*groups):
        group = [m for g in groups for m in g]
        for kind, way, h, da, db, q in group:
            arrive(da, db)
            if kind == 2:
                m_copy(0, way, h, db).wait_recv()
        for kind, way, h, da, db, q in group:
            value = chip_sum(da, db, quarter(h, q))
            if kind == 2:
                value = value + get(mr, m_at(0, way, h, db))
            put(ms, m_at(kind, way, h, db), value)
        for kind, way, h, da, db, q in group:
            m_copy(kind, way, h, db).start()

    def n_copy(d, h):
        at = (d - 1) * 2 + h
        return pltpu.make_async_remote_copy(
            src_ref=ns.at[at],
            dst_ref=nr.at[at],
            send_sem=n_ss.at[at],
            recv_sem=n_rs.at[at],
            device_id=near_b[d],
            device_id_type=MESH,
        )

    sources = (((2, 0), (1, 1)), ((1, 0), (2, 1)))

    def first_wait(db, h):
        arrive(0, db)
        for q in range(2):
            for kind, way in sources[q]:
                m_copy(kind, way, h, db).wait_recv()

    def first_sum(db, h):
        sums = []
        for q in range(2):
            total = chip_sum(0, db, quarter(h, q))
            for kind, way in sources[q]:
                total = total + get(mr, m_at(kind, way, h, db))
            sums.append(total)
        return jnp.concatenate(sums, axis=0)

    def n_send(h, *dbs):
        for db in dbs:
            first_wait(db, h)
        for db in dbs:
            put(ns, (db - 1) * 2 + h, first_sum(db, h))
        for db in dbs:
            n_copy(db, h).start()

    compute(0)
    for cp in b_loads[9:]:
        cp.start()
    loads[2].start()
    loads[3].start()
    compute(1, 2)
    enter()
    d_copy(0).start()
    pass_token(4, 5)
    d_copy(1).start()
    d_copy(2).start()
    compute(3, 4)
    d_copy(3).start()
    d_copy(4).start()
    send(m1(0, 2), m1(1, 2))
    step(5, 6)
    panel_one()
    send(m1(0, 1), m1(0, 3))
    step(7, 8)
    step(9, 10)
    send(m1(0, 0), m2(0, 2), m1(1, 1))
    pass_token(3, 6)
    step(11, 12)
    send(m2(0, 1), m2(0, 3), m1(1, 3))
    panel_two()
    send(m3(0, 2), m1(1, 0))
    step(13, 14)
    send(m3(0, 1), m2(1, 2))
    pass_token(2, 7)
    step(15)
    panel_three()
    send(m3(0, 3))
    send(m3(1, 2), m2(1, 1), m2(1, 3))
    send(m2(0, 0), m3(0, 0))
    panel_four()
    pass_token(1, -1)
    n_send(0, 2)
    send(m3(1, 1), m3(1, 3), m2(1, 0))
    n_send(0, 1, 3)
    send(m3(1, 0))
    panel_gather()
    n_send(1, 2)
    n_send(1, 1, 3)

    def z_copy(d, h):
        at = d * 2 + h
        return pltpu.make_async_remote_copy(
            src_ref=zs.at[h],
            dst_ref=zr.at[h],
            send_sem=z_ss.at[at],
            recv_sem=z_rs.at[h],
            device_id=(y, d, col),
            device_id_type=MESH,
        )

    def final_sum(h):
        first_wait(0, h)
        for d in (1, 2, 3):
            n_copy(d, h).wait_recv()
        total = first_sum(0, h)
        for d in (1, 2, 3):
            total = total + get(nr, (d - 1) * 2 + h)
        return anc[rows(h), :] - total

    relay = (z == 1) | (z == 3) | (z == 7)
    relay_copy = pltpu.make_async_remote_copy(
        src_ref=zr.at[0],
        dst_ref=zr.at[0],
        send_sem=z_ss.at[0],
        recv_sem=z_rs.at[0],
        device_id=(y, jnp.where(z == 7, 6, z + 1), col),
        device_id_type=MESH,
    )

    @pl.when(relay)
    def _():
        z_copy(0, 0).wait_recv()
        relay_copy.start()

    panel_use()
    for h in range(2):
        out[rows(h), :] = final_sum(h)

        @pl.when(z == 0)
        def _():
            put(zs, h, out[rows(h), :])
            if h == 0:
                pl.semaphore_wait(token, 2)
            for d in FIRST if h == 0 else FAR:
                z_copy(d, h).start()

    in_panel = (y == 0) & (col < 4)

    @pl.when(z == 0)
    def _():
        loads[2].wait()
        loads[3].wait()

        @pl.when(jnp.logical_not(in_panel))
        def _():
            out[...] = dot3(split(lin[...]), split(out[...]))

        for h in range(2):
            for d in FIRST if h == 0 else FAR:
                z_copy(d, h).wait_send()

    @pl.when(inner)
    def _():
        @pl.when(jnp.logical_not(relay))
        def _():
            z_copy(0, 0).wait_recv()

        @pl.when(in_panel)
        def _():
            z_copy(0, 1).wait_recv()
            out[...] = fp[:, pl.ds(pl.multiple_of(col * 128, 128), 128)]

        @pl.when(jnp.logical_not(in_panel))
        def _():
            for h in range(2):
                if h == 1:
                    z_copy(0, 1).wait_recv()
                w = (wh[:, rows(h)], wl[:, rows(h)])
                out[...] -= dot3(w, split(get(zr, h)))

        @pl.when(relay)
        def _():
            relay_copy.wait_send()

        px_copy.wait_send()
        agp_copy.wait_send()

        for stage in range(4):
            for d in (1, 2, 3):
                p_copy(stage, d).wait_send()

    for k in range(16):
        d_copy(k).wait_send()
    for at in range(48):
        m_copy(at // 16, at // 8 % 2, at // 4 % 2, at % 4).wait_send()
    for d in range(1, 4):
        for h in range(2):
            n_copy(d, h).wait_send()


def shards(lower, upper, pattern, ancestor, lower_inverse, upper_inverse):
    f32, bf16, i16 = jnp.float32, jnp.bfloat16, jnp.int16
    vmem, dma = pltpu.VMEM, pltpu.SemaphoreType.DMA
    hbm = pl.BlockSpec(memory_space=pl.ANY)
    msg = HALF + 16
    return pl.pallas_call(
        kernel,
        out_shape=pltpu.VMEM((ROWS, 128), f32),
        in_specs=[hbm] * 6,
        out_specs=pl.BlockSpec(memory_space=pltpu.VMEM),
        scratch_shapes=[
            pltpu.SMEM((6, 1, 32), jnp.int32),
            vmem((ROWS, KS), bf16),
            vmem((16, KS, 256), bf16),
            vmem((2, KS, 256), bf16),
            vmem((ROWS, 128), f32),
            vmem((NB, NB), f32),
            vmem((NB, NB), f32),
            vmem((2, 16, ROWS, 128), f32),
            vmem((16, ROWS, 128), f32),
            vmem((48, QUARTER + 16, 128), i16),
            vmem((48, QUARTER + 16, 128), i16),
            vmem((6, msg, 128), i16),
            vmem((6, msg, 128), i16),
            vmem((2, msg, 128), i16),
            vmem((2, msg, 128), i16),
            vmem((ROWS, NB), f32),
            vmem((HALF, NB), f32),
            vmem((16, 80, 128), i16),
            vmem((16, 80, 128), i16),
            vmem((16, 80, 128), i16),
            vmem((16, 80, 128), i16),
            vmem((ROWS, NB), f32),
            vmem((ROWS, NB), bf16),
            vmem((ROWS, NB), bf16),
            dma((5,)),
            dma((18,)),
            dma((16,)),
            dma((16,)),
            dma((48,)),
            dma((48,)),
            dma((6,)),
            dma((6,)),
            dma((16,)),
            dma((2,)),
            dma((2,)),
            dma((12,)),
            dma((12,)),
            dma((2,)),
            pltpu.SemaphoreType.REGULAR,
        ],
        compiler_params=pltpu.CompilerParams(
            collective_id=0, has_side_effects=True, vmem_limit_bytes=56 * 2**20
        ),
    )(jnp.transpose(pattern, (2, 0, 1)), lower, upper, ancestor, lower_inverse, upper_inverse)


def solution(mesh):
    in_specs = (
        P("layer", "row", "col"),
        P("layer", "col", None),
        P("layer", None, None),
        P("row", ("layer", "col")),
        P(),
        P(),
    )
    out_specs = P("row", ("layer", "col"))
    return jax.shard_map(shards, mesh=mesh, in_specs=in_specs, out_specs=out_specs, check_vma=False)
```

```python
import math

import jax
import jax.numpy as jnp
from jax import lax
from jax.experimental import pallas as pl
from jax.experimental.pallas import tpu as pltpu
from jax.sharding import PartitionSpec as P

MESH = pl.DeviceIdType.MESH
SNW = 2048
BLK = 128
NX, NY, NZ = 4, 4, 8
ROWS = 512
HALF = 256
QUARTER = 128
KS = 1536
NB = 512
ORDER = (
    (2, 2),
    (2, 1), (1, 2),
    (2, 3), (3, 2),
    (2, 0), (0, 2),
    (1, 1), (3, 3),
    (1, 3), (3, 1),
    (1, 0), (0, 1),
    (3, 0), (0, 3),
    (0, 0),
)
FIRST = (1, 7, 3, 5)
FAR = (3, 5, 1, 7, 2, 6, 4)
STEP = 16.0 / math.log(2.0)
TOP = 32700.0


def scale_code(x):
    top = jnp.max(jnp.abs(x), axis=0, keepdims=True)
    return jnp.ceil(jnp.log(jnp.maximum(top, 1e-30)) * STEP)


def encode(x, code):
    return jnp.round(x * (jnp.exp(code * (-1.0 / STEP)) * TOP)).astype(jnp.int32).astype(jnp.int16)


def scale_of(code):
    return jnp.exp(code * (1.0 / STEP)) * (1.0 / TOP)


def widen(q):
    return q.astype(jnp.int32).astype(jnp.float32)


def put(ref, at, x):
    n = x.shape[0]
    code = scale_code(x)
    ref[at, :n, :] = encode(x, code)
    ref[at, n:, :] = jnp.broadcast_to(code, (16, x.shape[1])).astype(jnp.int32).astype(jnp.int16)


def get(ref, at):
    n = ref.shape[1] - 16
    code = widen(ref[at, n:, :])[:1]
    return widen(ref[at, :n, :]) * scale_of(code)


def put_wide(ref, at, x):
    row = lax.broadcasted_iota(jnp.int32, (16, 128), 0) % 4
    codes = jnp.zeros((16, 128), jnp.float32)
    for g in range(4):
        part = x[:, g * 128 : (g + 1) * 128]
        code = scale_code(part)
        ref[at, g * 16 : (g + 1) * 16, :] = encode(part, code)
        codes = jnp.where(row == g, jnp.broadcast_to(code, (16, 128)), codes)
    ref[at, 64:, :] = codes.astype(jnp.int32).astype(jnp.int16)


def get_wide(ref, at):
    scales = scale_of(widen(ref[at, 64:, :]))
    return [widen(ref[at, g * 16 : (g + 1) * 16, :]) * scales[g : g + 1] for g in range(4)]


def split(x):
    hi = x.astype(jnp.bfloat16)
    return hi, (x - hi.astype(jnp.float32)).astype(jnp.bfloat16)


def dot3(a, b):
    (ah, al), (bh, bl) = a, b
    dot = lambda u, v: jnp.dot(u, v, preferred_element_type=jnp.float32)
    return dot(ah, bh) + (dot(ah, bl) + dot(al, bh))


def kernel(
    pattern_in, lower, upper, ancestor, linv, uinv, out,
    pattern, a_ref, b_ref, bp_ref, anc, lin, uin, parts, peer,
    ms, mr, ns, nr, zs, zr,
    pp, px, ps, pr, agr, agp, fp, wh, wl,
    in_sem, b_sem, d_ss, d_rs, m_ss, m_rs, n_ss, n_rs, z_ss, z_rs,
    px_sem, p_ss, p_rs, agp_sem, token,
):
    y, z, col = (lax.axis_index(k) for k in ("layer", "row", "col"))
    x, c = col >> 1, col & 1
    other = 1 - c
    inner = z > 0

    def dev(dy, dx):
        return ((y + dy) & 3, z, ((x + dx) & 3) * 2 + c)

    near_a = {d: dev(c * d, other * d) for d in (1, -1)}
    near_b = {d: dev(other * d, c * d) for d in (1, 2, 3)}

    twin = (y, z, x * 2 + other)

    up, down = (y, (z + 1) & (NZ - 1), col), (y, (z - 1) & (NZ - 1), col)

    loads = [
        pltpu.make_async_copy(lower.at[0], a_ref, in_sem.at[0]),
        pltpu.make_async_copy(ancestor, anc, in_sem.at[1]),
        pltpu.make_async_copy(uinv, uin, in_sem.at[2]),
        pltpu.make_async_copy(linv, lin, in_sem.at[3]),
        pltpu.make_async_copy(pattern_in, pattern, in_sem.at[4]),
    ]
    b_loads = []
    for k, (dy, dx) in enumerate(ORDER):
        first = ((y + dy) & 3) * 1024 + ((x + dx) & 3) * 256
        b_loads.append(
            pltpu.make_async_copy(
                upper.at[0, :, pl.ds(pl.multiple_of(first, 256), 256)], b_ref.at[k], b_sem.at[k]
            )
        )
    bp_loads = [
        pltpu.make_async_copy(upper.at[0, :, q * 256 : (q + 1) * 256], bp_ref.at[q], b_sem.at[16 + q])
        for q in range(2)
    ]
    barrier = pltpu.get_barrier_semaphore()
    partners = [twin] + [dev(0, d) for d in (1, 2, 3)] + [dev(d, 0) for d in (1, 2, 3)]
    partners += [up, down]
    for partner in partners:
        pl.semaphore_signal(barrier, inc=1, device_id=partner, device_id_type=MESH)

    loads[0].start()
    loads[4].start()

    @pl.when(inner)
    def _():
        for cp in bp_loads:
            cp.start()

    for cp in b_loads[:3]:
        cp.start()
    loads[1].start()

    loads[4].wait()
    loads[0].wait()
    for cp in b_loads[3:9]:
        cp.start()
    for rb in range(ROWS // BLK):
        for kb in range(KS // 512):
            node = (col * KS + kb * 512) // SNW
            keep = pattern[node, 0, z * (ROWS // BLK) + rb].astype(jnp.float32)
            at = (slice(rb * BLK, (rb + 1) * BLK), slice(kb * 512, (kb + 1) * 512))
            a_ref[at] = (a_ref[at].astype(jnp.float32) * keep).astype(jnp.bfloat16)

    loads[1].wait()

    @pl.when(inner)
    def _():
        for q in range(2):
            bp_loads[q].wait()
        for q in range(2):
            pp[:, q * 256 : (q + 1) * 256] = jnp.dot(
                a_ref[...], bp_ref[q], preferred_element_type=jnp.float32
            )

        @pl.when((y == 0) & (col < 4))
        def _():
            here = pl.ds(pl.multiple_of(col * 128, 128), 128)
            pp[:, here] -= anc[...]


    px_copy = pltpu.make_async_remote_copy(
        src_ref=pp.at[pl.ds(pl.multiple_of(other * HALF, HALF), HALF)],
        dst_ref=px,
        send_sem=px_sem.at[0],
        recv_sem=px_sem.at[1],
        device_id=twin,
        device_id_type=MESH,
    )

    def enter():
        pl.semaphore_wait(barrier, len(partners))

        @pl.when(inner)
        def _():
            px_copy.start()

    def pass_token(above, below):
        @pl.when(z == above)
        def _():
            if above < 4:
                pl.semaphore_wait(token, 1)
            pl.semaphore_signal(token, inc=1, device_id=down, device_id_type=MESH)

        @pl.when(z == below)
        def _():
            if below > 5:
                pl.semaphore_wait(token, 1)
            pl.semaphore_signal(token, inc=1, device_id=up, device_id_type=MESH)

    far_a = {d: dev(c * d, other * d) for d in (1, 2, 3)}
    ONE, TWO, BACK_TWO, BACK_ONE = range(4)

    def p_copy(stage, d):
        src, dst, partner = {
            ONE: (ps.at[pl.ds(d * 4, 4)], pr.at[pl.ds(d * 4, 4)], far_a[d]),
            TWO: (ps.at[d], pr.at[d], near_b[d]),
            BACK_TWO: (agr.at[0], agr.at[d], near_b[d]),
            BACK_ONE: (agr.at[pl.ds(0, 4)], agr.at[pl.ds(d * 4, 4)], far_a[d]),
        }[stage]
        at = stage * 3 + d - 1
        return pltpu.make_async_remote_copy(
            src_ref=src,
            dst_ref=dst,
            send_sem=p_ss.at[at],
            recv_sem=p_rs.at[at],
            device_id=partner,
            device_id_type=MESH,
        )

    agp_copy = pltpu.make_async_remote_copy(
        src_ref=agr,
        dst_ref=agp,
        send_sem=agp_sem.at[0],
        recv_sem=agp_sem.at[1],
        device_id=twin,
        device_id_type=MESH,
    )

    def chip_at(da, db, core):
        dy, dx = core * da + (1 - core) * db, core * db + (1 - core) * da
        return ((y + dy) & 3) * 4 + ((x + dx) & 3)

    def panel_slice(da, db):
        return px[pl.ds(pl.multiple_of(chip_at(da, db, c) * 16, 16), 16), :]

    def panel_one():
        @pl.when(inner)
        def _():
            px_copy.wait_recv()
            px[...] += pp[pl.ds(pl.multiple_of(c * HALF, HALF), HALF), :]
            for d in (2, 1, 3):
                for db in range(4):
                    put_wide(ps, d * 4 + db, panel_slice(d, db))
            for d in (2, 1, 3):
                p_copy(ONE, d).start()

    def panel_two():
        @pl.when(inner)
        def _():
            for d in (1, 2, 3):
                p_copy(ONE, d).wait_recv()
            for db in range(4):
                total = panel_slice(0, db)
                for d in (1, 2, 3):
                    total = total + jnp.concatenate(get_wide(pr, d * 4 + db), axis=1)
                if db == 0:
                    fp[:16] = total
                else:
                    put_wide(ps, db, total)
            for d in (2, 1, 3):
                p_copy(TWO, d).start()

    def panel_three():
        @pl.when(inner)
        def _():
            for d in (1, 2, 3):
                p_copy(TWO, d).wait_recv()
            total = fp[:16]
            for d in (1, 2, 3):
                total = total + jnp.concatenate(get_wide(pr, d), axis=1)
            put_wide(agr, 0, -total)
            for d in (2, 1, 3):
                p_copy(BACK_TWO, d).start()

    def panel_four():
        @pl.when(inner)
        def _():
            for d in (1, 2, 3):
                p_copy(BACK_TWO, d).wait_recv()
            for d in (2, 1, 3):
                p_copy(BACK_ONE, d).start()

    def panel_gather():
        @pl.when(inner)
        def _():
            for d in (1, 2, 3):
                p_copy(BACK_ONE, d).wait_recv()
            agp_copy.start()

    def panel_use():
        @pl.when(inner)
        def _():
            def unpack(ref, core):
                for s in range(16):
                    at = pl.multiple_of(core * HALF + chip_at(-(s // 4), -(s % 4), core) * 16, 16)
                    for g, part in enumerate(get_wide(ref, s)):
                        fp[pl.ds(at, 16), g * 128 : (g + 1) * 128] = part

            unpack(agr, c)
            agp_copy.wait_recv()
            unpack(agp, other)
            loads[2].wait()
            loads[3].wait()
            panel = dot3(split(fp[...]), split(uin[...]))
            fp[...] = panel
            w = dot3(split(panel), split(lin[...]))
            wh[...], wl[...] = split(w)

    def slots(k):
        dy, dx = ORDER[k]
        return dx * 4 + dy, dy * 4 + dx

    def d_copy(k):
        s0, s1 = slots(k)
        s = jnp.where(c == 0, s1, s0)
        return pltpu.make_async_remote_copy(
            src_ref=parts.at[other, s],
            dst_ref=peer.at[s],
            send_sem=d_ss.at[s],
            recv_sem=d_rs.at[s],
            device_id=twin,
            device_id_type=MESH,
        )

    def compute(*ks):
        for k in ks:
            b_loads[k].wait()
        tiles = 2 // len(ks)
        for k in ks:
            s0, s1 = slots(k)
            for t in range(tiles):
                at = slice(t * ROWS // tiles, (t + 1) * ROWS // tiles)
                both = jnp.dot(a_ref[at], b_ref[k], preferred_element_type=jnp.float32)
                parts[0, s0, at] = both[:, :128]
                parts[1, s1, at] = both[:, 128:]

    def step(*ks):
        compute(*ks)
        for k in ks:
            d_copy(k).start()

    here = set()

    def arrive(da, db):
        s = da * 4 + db
        if s not in here:
            here.add(s)
            pltpu.make_async_copy(peer.at[s], peer.at[s], d_rs.at[s]).wait()

    def chip_sum(da, db, at):
        s = da * 4 + db
        return parts[c, s, at, :] + peer[s, at, :]

    def rows(h):
        return slice(h * HALF, (h + 1) * HALF)

    def quarter(h, q):
        return slice(h * HALF + q * QUARTER, h * HALF + (q + 1) * QUARTER)

    def m_at(kind, way, h, db):
        return ((kind * 2 + way) * 2 + h) * 4 + db

    def m_copy(kind, way, h, db):
        at = m_at(kind, way, h, db)
        return pltpu.make_async_remote_copy(
            src_ref=ms.at[at],
            dst_ref=mr.at[at],
            send_sem=m_ss.at[at],
            recv_sem=m_rs.at[at],
            device_id=near_a[1 if way == 0 else -1],
            device_id_type=MESH,
        )

    def m1(h, db):
        return [(0, 0, h, 2, db, 0), (0, 1, h, 2, db, 1)]

    def m2(h, db):
        return [(1, 0, h, 1, db, 1), (1, 1, h, 3, db, 0)]

    def m3(h, db):
        return [(2, 0, h, 1, db, 0), (2, 1, h, 3, db, 1)]

    def send(*groups):
        group = [m for g in groups for m in g]
        for kind, way, h, da, db, q in group:
            arrive(da, db)
            if kind == 2:
                m_copy(0, way, h, db).wait_recv()
        for kind, way, h, da, db, q in group:
            value = chip_sum(da, db, quarter(h, q))
            if kind == 2:
                value = value + get(mr, m_at(0, way, h, db))
            put(ms, m_at(kind, way, h, db), value)
        for kind, way, h, da, db, q in group:
            m_copy(kind, way, h, db).start()

    def n_copy(d, h):
        at = (d - 1) * 2 + h
        return pltpu.make_async_remote_copy(
            src_ref=ns.at[at],
            dst_ref=nr.at[at],
            send_sem=n_ss.at[at],
            recv_sem=n_rs.at[at],
            device_id=near_b[d],
            device_id_type=MESH,
        )

    sources = (((2, 0), (1, 1)), ((1, 0), (2, 1)))

    def first_wait(db, h):
        arrive(0, db)
        for q in range(2):
            for kind, way in sources[q]:
                m_copy(kind, way, h, db).wait_recv()

    def first_sum(db, h):
        sums = []
        for q in range(2):
            total = chip_sum(0, db, quarter(h, q))
            for kind, way in sources[q]:
                total = total + get(mr, m_at(kind, way, h, db))
            sums.append(total)
        return jnp.concatenate(sums, axis=0)

    def n_send(h, *dbs):
        for db in dbs:
            first_wait(db, h)
        for db in dbs:
            put(ns, (db - 1) * 2 + h, first_sum(db, h))
        for db in dbs:
            n_copy(db, h).start()

    compute(0)
    for cp in b_loads[9:]:
        cp.start()
    loads[2].start()
    loads[3].start()
    compute(1, 2)
    enter()
    d_copy(0).start()
    pass_token(4, 5)
    d_copy(1).start()
    d_copy(2).start()
    compute(3, 4)
    d_copy(3).start()
    d_copy(4).start()
    send(m1(0, 2), m1(1, 2))
    step(5, 6)
    panel_one()
    send(m1(0, 1), m1(0, 3))
    step(7, 8)
    step(9, 10)
    send(m1(0, 0), m2(0, 2), m1(1, 1))
    pass_token(3, 6)
    step(11, 12)
    send(m2(0, 1), m2(0, 3), m1(1, 3))
    panel_two()
    send(m3(0, 2), m1(1, 0))
    step(13, 14)
    send(m3(0, 1), m2(1, 2))
    pass_token(2, 7)
    step(15)
    panel_three()
    send(m3(0, 3))
    send(m3(1, 2), m2(1, 1), m2(1, 3))
    send(m2(0, 0), m3(0, 0))
    panel_four()
    pass_token(1, -1)
    n_send(0, 2)
    send(m3(1, 1), m3(1, 3), m2(1, 0))
    n_send(0, 1, 3)
    send(m3(1, 0))
    panel_gather()
    n_send(1, 2)
    n_send(1, 1, 3)

    def z_copy(d, h):
        at = d * 2 + h
        return pltpu.make_async_remote_copy(
            src_ref=zs.at[h],
            dst_ref=zr.at[h],
            send_sem=z_ss.at[at],
            recv_sem=z_rs.at[h],
            device_id=(y, d, col),
            device_id_type=MESH,
        )

    def final_sum(h):
        first_wait(0, h)
        for d in (1, 2, 3):
            n_copy(d, h).wait_recv()
        total = first_sum(0, h)
        for d in (1, 2, 3):
            total = total + get(nr, (d - 1) * 2 + h)
        return anc[rows(h), :] - total

    relay = (z == 1) | (z == 3) | (z == 7)
    relay_copy = pltpu.make_async_remote_copy(
        src_ref=zr.at[0],
        dst_ref=zr.at[0],
        send_sem=z_ss.at[0],
        recv_sem=z_rs.at[0],
        device_id=(y, jnp.where(z == 7, 6, z + 1), col),
        device_id_type=MESH,
    )

    @pl.when(relay)
    def _():
        z_copy(0, 0).wait_recv()
        relay_copy.start()

    panel_use()
    for h in range(2):
        out[rows(h), :] = final_sum(h)

        @pl.when(z == 0)
        def _():
            put(zs, h, out[rows(h), :])
            if h == 0:
                pl.semaphore_wait(token, 2)
            for d in FIRST if h == 0 else FAR:
                z_copy(d, h).start()

    in_panel = (y == 0) & (col < 4)

    @pl.when(z == 0)
    def _():
        loads[2].wait()
        loads[3].wait()

        @pl.when(jnp.logical_not(in_panel))
        def _():
            out[...] = dot3(split(lin[...]), split(out[...]))

        for h in range(2):
            for d in FIRST if h == 0 else FAR:
                z_copy(d, h).wait_send()

    @pl.when(inner)
    def _():
        @pl.when(jnp.logical_not(relay))
        def _():
            z_copy(0, 0).wait_recv()

        @pl.when(in_panel)
        def _():
            z_copy(0, 1).wait_recv()
            out[...] = fp[:, pl.ds(pl.multiple_of(col * 128, 128), 128)]

        @pl.when(jnp.logical_not(in_panel))
        def _():
            for h in range(2):
                if h == 1:
                    z_copy(0, 1).wait_recv()
                w = (wh[:, rows(h)], wl[:, rows(h)])
                out[...] -= dot3(w, split(get(zr, h)))

        @pl.when(relay)
        def _():
            relay_copy.wait_send()

        px_copy.wait_send()
        agp_copy.wait_send()

        for stage in range(4):
            for d in (1, 2, 3):
                p_copy(stage, d).wait_send()

    for k in range(16):
        d_copy(k).wait_send()
    for at in range(48):
        m_copy(at // 16, at // 8 % 2, at // 4 % 2, at % 4).wait_send()
    for d in range(1, 4):
        for h in range(2):
            n_copy(d, h).wait_send()


def shards(lower, upper, pattern, ancestor, lower_inverse, upper_inverse):
    f32, bf16, i16 = jnp.float32, jnp.bfloat16, jnp.int16
    vmem, dma = pltpu.VMEM, pltpu.SemaphoreType.DMA
    hbm = pl.BlockSpec(memory_space=pl.ANY)
    msg = HALF + 16
    return pl.pallas_call(
        kernel,
        out_shape=pltpu.VMEM((ROWS, 128), f32),
        in_specs=[hbm] * 6,
        out_specs=pl.BlockSpec(memory_space=pltpu.VMEM),
        scratch_shapes=[
            pltpu.SMEM((6, 1, 32), jnp.int32),
            vmem((ROWS, KS), bf16),
            vmem((16, KS, 256), bf16),
            vmem((2, KS, 256), bf16),
            vmem((ROWS, 128), f32),
            vmem((NB, NB), f32),
            vmem((NB, NB), f32),
            vmem((2, 16, ROWS, 128), f32),
            vmem((16, ROWS, 128), f32),
            vmem((48, QUARTER + 16, 128), i16),
            vmem((48, QUARTER + 16, 128), i16),
            vmem((6, msg, 128), i16),
            vmem((6, msg, 128), i16),
            vmem((2, msg, 128), i16),
            vmem((2, msg, 128), i16),
            vmem((ROWS, NB), f32),
            vmem((HALF, NB), f32),
            vmem((16, 80, 128), i16),
            vmem((16, 80, 128), i16),
            vmem((16, 80, 128), i16),
            vmem((16, 80, 128), i16),
            vmem((ROWS, NB), f32),
            vmem((ROWS, NB), bf16),
            vmem((ROWS, NB), bf16),
            dma((5,)),
            dma((18,)),
            dma((16,)),
            dma((16,)),
            dma((48,)),
            dma((48,)),
            dma((6,)),
            dma((6,)),
            dma((16,)),
            dma((2,)),
            dma((2,)),
            dma((12,)),
            dma((12,)),
            dma((2,)),
            pltpu.SemaphoreType.REGULAR,
        ],
        compiler_params=pltpu.CompilerParams(
            collective_id=0, has_side_effects=True, vmem_limit_bytes=56 * 2**20
        ),
    )(jnp.transpose(pattern, (2, 0, 1)), lower, upper, ancestor, lower_inverse, upper_inverse)


def solution(mesh):
    in_specs = (
        P("layer", "row", "col"),
        P("layer", "col", None),
        P("layer", None, None),
        P("row", ("layer", "col")),
        P(),
        P(),
    )
    out_specs = P("row", ("layer", "col"))
    return jax.shard_map(shards, mesh=mesh, in_specs=in_specs, out_specs=out_specs, check_vma=False)
```
